128 devices in a mesh: section: 2 (over core), dp: 16 (over x, y), heads: 4 (over z).
Axes of the slice: x: 4, y: 4, z: 4, core: 2. Of those that a mesh axis runs over, the one named last changes fastest.
Arguments:
- patches: bfloat16 [12544, 768], P('dp'), may hold values from -6 to 6
- mask_flags: int32 [64, 196], P('dp'), may hold values 0 or 1
- image_tags: int32 [64], P('dp'), may hold values from 0 to 7
- mask_token: float32 [768], replicated, may hold values from -6 to 6
- group_table: float32 [8, 768], replicated, may hold values from -3 to 3
- qkv_weight: float32 [2, 768, 3, 768], P('section', 'dp'), may hold values from -0.21875 to 0.21875
- query_value_bias: float32 [2, 2, 768], P('section'), may hold values from -3 to 3
- out_weight: float32 [2, 768, 768], P('section', None, 'dp'), may hold values from -0.625 to 0.625
- up_weight: float32 [2, 768, 3072], P('section', 'dp'), may hold values from -0.21875 to 0.21875
- hidden_bias: float32 [2, 3072], P('section'), may hold values from -3 to 3
- down_weight: float32 [2, 3072, 768], P('section', None, 'dp'), may hold values from -0.109375 to 0.109375
- norm_gains: float32 [2, 2, 768], P('section'), may hold values from 0.5 to 1.5
- norm_biases: float32 [2, 4, 768], P('section'), may hold values from -2 to 2
- cotangent: bfloat16 [12544, 768], P('dp'), may hold values from -6 to 6
Outputs:
- stream_ends: float32 [2, 12544, 768], P('section', 'dp')
- grad_qkv: float32 [2, 768, 3, 768], P('section', 'dp')
- grad_qv_bias: float32 [2, 2, 768], P('section')
- grad_out: float32 [2, 768, 768], P('section', None, 'dp')
- grad_up: float32 [2, 768, 3072], P('section', 'dp')
- grad_hidden_bias: float32 [2, 3072], P('section')
- grad_down: float32 [2, 3072, 768], P('section', None, 'dp')
- grad_gains: float32 [2, 2, 768], P('section')
- grad_biases: float32 [2, 4, 768], P('section')
- grad_token: float32 [768], P('section')
- grad_table: float32 [8, 768], P(None, 'section')
The draws below stay inside these ranges and needn't reach their ends.
Inputs may be any that keep to these rules, and one draw needn't show every extreme that they name: `image_tags`: the dataset group of each image; micro-batch (group mod 2) sizes may differ from device to device. `mask_flags`: 1 marks a masked patch.
All inputs are finite; a program needn't handle non-finite values. No bound on the sum of `mask_flags` on one device may be relied on, other than what follows from the above.
Results may differ from the reference program's by a relative error of at most 0.013.
Values may be sent and summed in bfloat16 or wider, within the bound.
No kernel may reach another device: no remote copies, remote signals or barrier semaphores. Data moves between devices by JAX's collectives and lax.ppermute only.
A program may use at most 192 MiB of HBM per device.

```python
import jax
import jax.numpy as jnp
from jax import lax

D = 768
HEADS = 12
HD = 64
FF = 3072
PATCHES = 196
GROUPS = 8
IMAGES = 64
TOKENS = 12544


def place_ends(result, stream_key, low, top_value):
    longest = result.shape.index(max(result.shape))
    spots = []
    for shift in (0, 1):
        where = [jax.random.randint(jax.random.fold_in(stream_key, axis), (), 0, length) for axis, length in enumerate(result.shape)]
        where[longest] = (where[longest] + shift) % result.shape[longest]
        spots.append(tuple(where))
    return result.at[spots[0]].set(low).at[spots[1]].set(top_value)


def shard_levels(stream_key, extent, cuts, least, high):
    loudness, own = 1.0, jax.random.fold_in(stream_key, 6)
    for axis_at, shards_of in cuts:
        draws = jnp.exp(jax.random.uniform(jax.random.fold_in(own, axis_at), (shards_of,), jnp.float32, least / len(cuts), high / len(cuts)))
        loudness = loudness * jnp.repeat(draws, extent[axis_at] // shards_of).reshape([-1 if axis == axis_at else 1 for axis in range(len(extent))])
    return loudness


def noise(rng, shape, spread, bound, cuts=(), kind=jnp.bfloat16):
    entries = jax.random.normal(rng, shape, jnp.float32) * spread
    if len(cuts) > 0:
        entries = shard_levels(rng, shape, cuts, -0.22, 0.18) * entries
    return jnp.clip(entries, min=-bound, max=bound).astype(kind)


def setup_inputs(seed: int = 0) -> dict:
    arg_keys = jax.random.split(jax.random.key(seed), 15)
    patches = noise(arg_keys[0], (TOKENS, D), 1.0, 6.0, ((0, 16),))
    mask_flags = place_ends((jax.random.randint(arg_keys[1], (IMAGES, PATCHES), 0, 5) < 3).astype(jnp.int32), jax.random.fold_in(arg_keys[1], 1), 0, 1)
    image_tags = place_ends(jax.random.randint(arg_keys[2], (IMAGES,), 0, GROUPS), jax.random.fold_in(arg_keys[2], 1), 0, GROUPS - 1).astype(jnp.int32)
    mask_token = noise(arg_keys[3], (D,), 1.0, 6.0, (), jnp.float32)
    group_table = noise(arg_keys[4], (GROUPS, D), 0.5, 3.0, (), jnp.float32)
    qkv_weight = noise(arg_keys[5], (2, D, 3, HEADS * HD), D ** -0.5, 0.21875, ((0, 2), (1, 16)), jnp.float32)
    query_value_bias = noise(arg_keys[6], (2, 2, HEADS * HD), 0.5, 3.0, ((0, 2),), jnp.float32)
    out_weight = noise(arg_keys[7], (2, HEADS * HD, D), (HEADS * HD // 8) ** -0.5, 0.625, ((0, 2), (2, 16)), jnp.float32)
    up_weight = noise(arg_keys[8], (2, D, FF), D ** -0.5, 0.21875, ((0, 2), (1, 16)), jnp.float32)
    hidden_bias = noise(arg_keys[9], (2, FF), 0.5, 3.0, ((0, 2),), jnp.float32)
    down_weight = noise(arg_keys[10], (2, FF, D), FF ** -0.5, 0.109375, ((0, 2), (2, 16)), jnp.float32)
    norm_gains = jnp.clip(1.0 + 0.1 * jax.random.normal(arg_keys[11], (2, 2, D), jnp.float32), 0.5, 1.5)
    norm_biases = noise(arg_keys[12], (2, 4, D), 0.3, 2.0, ((0, 2),), jnp.float32)
    cotangent = noise(arg_keys[13], (TOKENS, D), 1.0, 6.0, ((0, 16),))
    return dict(patches=patches, mask_flags=mask_flags, image_tags=image_tags, mask_token=mask_token, group_table=group_table, qkv_weight=qkv_weight, query_value_bias=query_value_bias, out_weight=out_weight, up_weight=up_weight, hidden_bias=hidden_bias, down_weight=down_weight, norm_gains=norm_gains, norm_biases=norm_biases, cotangent=cotangent)


@jax.custom_vjp
def low(v):
    return lax.optimization_barrier(v.astype(jnp.bfloat16)).astype(jnp.float32)

@jax.custom_vjp
def low_back(v):
    return v

def low_keep(v):
    return (low(v), None)

def low_pass(kept, grad):
    return (grad,)

def back_keep(v):
    return (v, None)

def back_low(kept, grad):
    return (low(grad),)
low.defvjp(low_keep, low_pass)
low_back.defvjp(back_keep, back_low)
highest = lax.Precision.HIGHEST
epsilon = 1e-06

def product(left, right):
    return jnp.dot(left, right, precision=highest, preferred_element_type=jnp.float32)

def normalize(stream, gain, shift):
    average = lax.optimization_barrier(jnp.mean(stream, axis=-1, keepdims=True))
    centred = stream - average
    variance = lax.optimization_barrier(jnp.mean(centred * centred, axis=-1, keepdims=True))
    return centred * lax.rsqrt(variance + epsilon) * gain + shift

def layer_pass(stream, qkv_weight, qv_bias, out_weight, up_weight, hidden_bias, down_weight, gains, biases):
    row_count = stream.shape[0]
    image_count = row_count // PATCHES
    feature_width = out_weight.shape[0]
    normed = low(normalize(stream, gains[0], biases[0]))
    packed = jnp.einsum('nd,dcf->ncf', normed, qkv_weight, precision=highest)
    offset = jnp.stack([qv_bias[0], jnp.zeros_like(qv_bias[0]), qv_bias[1]])
    packed = low_back(low(packed + offset[None]))
    split_parts = packed.reshape(image_count, PATCHES, 3, feature_width // HD, HD)
    queries = split_parts[:, :, 0]
    key_rows = split_parts[:, :, 1]
    valued = split_parts[:, :, 2]
    scores = jnp.einsum('iqhd,ikhd->ihqk', queries, key_rows, precision=highest) * HD ** (-0.5)
    scores = low_back(scores)
    attn_probs = low(jax.nn.softmax(scores, axis=-1))
    context = jnp.einsum('ihqk,ikhd->iqhd', attn_probs, valued, precision=highest)
    context = low_back(low(context.reshape(row_count, feature_width)))
    middle = stream + low_back(product(context, out_weight) + biases[1])
    normed_two = low(normalize(middle, gains[1], biases[2]))
    up_value = low_back(product(normed_two, up_weight) + hidden_bias)
    hidden = low(jax.nn.gelu(up_value, approximate=False))
    return middle + low_back(product(hidden, down_weight) + biases[3])

def reference(patches, mask_flags, image_tags, mask_token, group_table, qkv_weight, query_value_bias, out_weight, up_weight, hidden_bias, down_weight, norm_gains, norm_biases, cotangent):
    per_block = 16
    blocks = IMAGES // per_block
    block_rows = per_block * PATCHES
    flag_blocks = mask_flags.reshape(blocks, block_rows, 1)
    tag_blocks = image_tags.reshape(blocks, per_block)

    def whole(inputs_full, token_row, table_rows, weight_qkv, bias_qv, weight_out, weight_up, bias_hidden, weight_down, gain_rows, bias_rows):
        weight_qkv = low(weight_qkv)
        weight_out = low(weight_out)
        weight_up = low(weight_up)
        weight_down = low(weight_down)

        def one_block(pieces):
            block_in, flags, labels = pieces
            onehot = (labels[:, None] == jnp.arange(GROUPS, dtype=jnp.int32)[None, :]).astype(jnp.float32)
            per_image = product(onehot, table_rows)
            stream = jnp.where(flags > 0, token_row[None, :], block_in) + jnp.repeat(per_image, PATCHES, axis=0)
            between = layer_pass(stream, weight_qkv[0], bias_qv[0], weight_out[0], weight_up[0], bias_hidden[0], weight_down[0], gain_rows[0], bias_rows[0])
            between = low_back(low(between))
            return layer_pass(between, weight_qkv[1], bias_qv[1], weight_out[1], weight_up[1], bias_hidden[1], weight_down[1], gain_rows[1], bias_rows[1])
        outputs = lax.map(jax.checkpoint(one_block), (inputs_full.reshape(blocks, block_rows, D), flag_blocks, tag_blocks))
        return outputs.reshape(TOKENS, D)
    final_out, pullback = jax.vjp(whole, patches.astype(jnp.float32), mask_token, group_table, qkv_weight, query_value_bias, out_weight, up_weight, hidden_bias, down_weight, norm_gains, norm_biases)
    all_grads = pullback(cotangent.astype(jnp.float32))
    stream_ends = jnp.stack([all_grads[0], final_out])
    return (stream_ends, all_grads[3], all_grads[4], all_grads[5], all_grads[6], all_grads[7], all_grads[8], all_grads[9], all_grads[10], all_grads[1], all_grads[2])
```

```python
import jax
import jax.numpy as jnp
from jax import lax
from jax.sharding import PartitionSpec as P

D = 768
HD = 64
FF = 3072
PATCHES = 196
GROUPS = 8
HALF = D // 2
HALF_FF = FF // 2
epsilon = 1e-06
highest = lax.Precision.HIGHEST
SWAP = [(0, 1), (1, 0)]

WIDTHS = (3 * HALF, HALF, HALF_FF, HALF_FF)
LAYER = sum(WIDTHS)


def swap(value):
    return lax.ppermute(value, "section", SWAP)


def both_cores(part):
    return part + swap(part.astype(jnp.bfloat16)).astype(jnp.float32)


def normalize(stream, gain, shift):
    average = jnp.mean(stream, axis=-1, keepdims=True)
    centred = stream - average
    variance = jnp.mean(centred * centred, axis=-1, keepdims=True)
    return centred * lax.rsqrt(variance + epsilon) * gain + shift


def exact_gelu(up_value):
    return jax.nn.gelu(up_value, approximate=False)


def contract(form, left, right):
    return jnp.einsum(form, left, right, preferred_element_type=jnp.float32)


def layer_forward(stream, weights):
    weight_qkv, out_t, weight_up, down_t, bias_qv, bias_hidden, gain_rows, bias_rows = weights
    normed = normalize(stream, gain_rows[0], bias_rows[0]).astype(jnp.bfloat16)
    packed = contract("nd,df->nf", normed, weight_qkv)
    offset = jnp.concatenate([bias_qv[0], jnp.zeros_like(bias_qv[0]), bias_qv[1]])
    packed = (packed + offset[None]).astype(jnp.bfloat16)
    split_parts = packed.reshape(PATCHES, 3, HALF // HD, HD)
    queries, key_rows, valued = split_parts[:, 0], split_parts[:, 1], split_parts[:, 2]
    scores = contract("qhd,khd->hqk", queries, key_rows) * HD ** (-0.5)
    summit = jnp.max(scores, axis=-1, keepdims=True)
    raised = jnp.exp(scores - summit)
    totals = jnp.sum(raised, axis=-1, keepdims=True)
    log_total = summit + jnp.log(totals)
    attn_probs = (raised / totals).astype(jnp.bfloat16)
    context = contract("hqk,khd->qhd", attn_probs, valued).reshape(PATCHES, HALF).astype(jnp.bfloat16)
    attended = both_cores(contract("nh,dh->nd", context, out_t))
    middle = stream + (attended + bias_rows[1])
    normed_two = normalize(middle, gain_rows[1], bias_rows[2]).astype(jnp.bfloat16)
    up_value = contract("nd,df->nf", normed_two, weight_up) + bias_hidden
    hidden = exact_gelu(up_value).astype(jnp.bfloat16)
    mixed = both_cores(contract("nf,df->nd", hidden, down_t))
    result = middle + (mixed + bias_rows[3])
    kept = (stream, normed, queries, key_rows, valued, log_total, context, middle, normed_two, up_value, hidden)
    return result, kept


def layer_backward(grad_output, kept, weights):
    stream, normed, queries, key_rows, valued, log_total, context, middle, normed_two, up_value, hidden = kept
    weight_qkv, out_t, weight_up, down_t, bias_qv, bias_hidden, gain_rows, bias_rows = weights
    scale = HD ** (-0.5)
    grad_branch = grad_output.astype(jnp.bfloat16)
    grad_down = contract("nd,nf->df", grad_branch, hidden)
    bias_down = jnp.sum(grad_branch.astype(jnp.float32), axis=0)
    grad_hidden = contract("nd,df->nf", grad_branch, down_t)
    grad_upper = jax.vjp(exact_gelu, up_value)[1](grad_hidden)[0].astype(jnp.bfloat16)
    grad_up = contract("nd,nf->df", normed_two, grad_upper)
    bias_up = jnp.sum(grad_upper.astype(jnp.float32), axis=0)
    grad_normed_two = both_cores(contract("nf,df->nd", grad_upper, weight_up))
    into_middle, gain_two, shift_two = jax.vjp(normalize, middle, gain_rows[1], bias_rows[2])[1](grad_normed_two)
    grad_middle = grad_output + into_middle
    grad_attn = grad_middle.astype(jnp.bfloat16)
    grad_out = contract("nd,nh->dh", grad_attn, context)
    bias_out = jnp.sum(grad_attn.astype(jnp.float32), axis=0)
    grad_context = contract("nd,dh->nh", grad_attn, out_t).astype(jnp.bfloat16).reshape(queries.shape)
    scores = contract("qhd,khd->hqk", queries, key_rows) * scale
    soft = jnp.exp(scores - log_total)
    grad_values = contract("hqk,qhd->khd", soft.astype(jnp.bfloat16), grad_context).astype(jnp.bfloat16)
    grad_probs = contract("qhd,khd->hqk", grad_context, valued)
    grad_scores = soft * (grad_probs - jnp.sum(grad_probs * soft, axis=-1, keepdims=True))
    grad_scores = grad_scores.astype(jnp.bfloat16)
    grad_queries = (contract("hqk,khd->qhd", grad_scores, key_rows) * scale).astype(jnp.bfloat16)
    grad_keys = (contract("hqk,qhd->khd", grad_scores, queries) * scale).astype(jnp.bfloat16)
    grad_packed = jnp.stack([grad_queries, grad_keys, grad_values], axis=1).reshape(PATCHES, 3 * HALF)
    grad_qkv = contract("nd,nf->df", normed, grad_packed)
    bias_query = jnp.sum(grad_packed[:, :HALF].astype(jnp.float32), axis=0)
    bias_value = jnp.sum(grad_packed[:, 2 * HALF :].astype(jnp.float32), axis=0)
    grad_normed = both_cores(contract("nf,df->nd", grad_packed, weight_qkv))
    into_stream, gain_one, shift_one = jax.vjp(normalize, stream, gain_rows[0], bias_rows[0])[1](grad_normed)
    grad_in = grad_middle + into_stream
    matrices = tuple(g.astype(jnp.bfloat16) for g in (grad_qkv, grad_out, grad_up, grad_down))
    whole_vectors = jnp.stack([gain_one, gain_two, shift_one, bias_out, shift_two, bias_down])
    half_vectors = jnp.concatenate([bias_query, bias_value, bias_up])
    return grad_in, matrices, whole_vectors, half_vectors


def per_device(
    patches, mask_flags, image_tags, mask_token, group_table, qkv_weight, query_value_bias, out_weight,
    up_weight, hidden_bias, down_weight, norm_gains, norm_biases, cotangent,
):
    place = lax.axis_index("heads")
    first = lax.axis_index("section") == 0

    rows = qkv_weight.shape[1]
    low = jnp.bfloat16
    pieces = (
        qkv_weight[0].astype(low).reshape(rows, 3, 2, HALF),
        out_weight[0].astype(low).T.reshape(rows, 1, 2, HALF),
        up_weight[0].astype(low).reshape(rows, 1, 2, HALF_FF),
        down_weight[0].astype(low).T.reshape(rows, 1, 2, HALF_FF),
    )
    halves = [jnp.concatenate([p[:, :, h].reshape(rows, -1) for p in pieces], axis=1) for h in (0, 1)]
    mine = jnp.where(first, halves[0], halves[1])
    other = swap(jnp.where(first, halves[1], halves[0]))
    shard = jnp.concatenate([jnp.where(first, mine, other), jnp.where(first, other, mine)], axis=1)
    joined = lax.all_gather(shard, "dp", axis=0, tiled=True)

    def half_of(vector):
        return jnp.where(first, vector[..., : vector.shape[-1] // 2], vector[..., vector.shape[-1] // 2 :])

    vectors = lax.all_gather(
        jnp.concatenate([norm_gains[0], norm_biases[0], query_value_bias[0], hidden_bias[0].reshape(4, D)]),
        "section", axis=0,
    )
    weights = []
    for layer in range(2):
        base = layer * LAYER
        parts = []
        for width in WIDTHS:
            parts.append(joined[:, base : base + width])
            base += width
        v = vectors[layer]
        weights.append((*parts, half_of(v[6:8]), half_of(v[8:12].reshape(FF)), v[0:2], v[2:6]))

    def own(rows_of):
        return lax.dynamic_slice_in_dim(rows_of, place * PATCHES, PATCHES, 0).astype(jnp.float32)

    masked = lax.dynamic_slice_in_dim(mask_flags, place, 1, 0).reshape(PATCHES, 1) > 0
    tag = lax.dynamic_slice_in_dim(image_tags, place, 1, 0)
    onehot = (tag[:, None] == jnp.arange(GROUPS, dtype=jnp.int32)[None, :]).astype(jnp.float32)
    image_row = jnp.sum(onehot.T * group_table, axis=0, keepdims=True)
    stream_zero = jnp.where(masked, mask_token[None, :], own(patches)) + image_row

    result, kept_zero = layer_forward(stream_zero, weights[0])
    stream_one = result.astype(low).astype(jnp.float32)
    final, kept_one = layer_forward(stream_one, weights[1])
    grad_one, matrices_one, whole_one, half_one = layer_backward(own(cotangent), kept_one, weights[1])
    grad_one = grad_one.astype(low).astype(jnp.float32)
    grad_zero, matrices_zero, whole_zero, half_zero = layer_backward(grad_one, kept_zero, weights[0])

    summed = lax.psum_scatter(
        jnp.concatenate(matrices_zero + matrices_one, axis=1), "dp", scatter_dimension=0, tiled=True
    )
    mine = jnp.where(first, summed[:, :LAYER], summed[:, LAYER:])
    other = swap(jnp.where(first, summed[:, LAYER:], summed[:, :LAYER]))
    layer_sums = jnp.concatenate([jnp.where(first, mine, other), jnp.where(first, other, mine)], axis=1)
    quarter = layer_sums.shape[1] // 4
    spread = jnp.stack([layer_sums[:, k * quarter : (k + 1) * quarter] for k in range(4)])
    spread = lax.all_to_all(spread, "heads", 0, 0, tiled=True)
    spread = jnp.sum(spread.astype(jnp.float32), axis=0).astype(low)
    total = lax.all_gather(spread, "heads", axis=0)
    total = jnp.concatenate([total[k] for k in range(4)], axis=1).astype(jnp.float32)
    outs = []
    base = 0
    for width in WIDTHS:
        outs.append((total[:, base : base + width], total[:, LAYER + base : LAYER + base + width]))
        base += width
    grad_qkv = jnp.concatenate([o.reshape(rows, 3, HALF) for o in outs[0]], axis=2)
    grad_out = jnp.concatenate(outs[1], axis=1).T
    grad_up = jnp.concatenate(outs[2], axis=1)
    grad_down = jnp.concatenate(outs[3], axis=1).T

    half_mine = jnp.where(first, half_zero, half_one)
    half_other = swap(jnp.where(first, half_one, half_zero))
    half_both = (jnp.where(first, half_mine, half_other), jnp.where(first, half_other, half_mine))
    qv = jnp.concatenate([h[: 2 * HALF].reshape(2, HALF) for h in half_both], axis=1)
    hid = jnp.concatenate([h[2 * HALF :] for h in half_both]).reshape(4, D)
    token = jnp.sum(jnp.where(masked, grad_zero, 0.0), axis=0)
    table = onehot.T * jnp.sum(grad_zero, axis=0)[None, :]
    ends = half_of(jnp.concatenate([token[None], table])).reshape(-1)
    ends = jnp.pad(ends, (0, 5 * D - ends.shape[0])).reshape(5, D)
    small = jnp.concatenate([jnp.where(first, whole_zero, whole_one), qv, hid, ends])
    small = jnp.sum(lax.all_gather(small, "heads", axis=0), axis=0)
    small = jnp.sum(lax.all_gather(small, "dp", axis=0), axis=0)
    ends = small[12:17].reshape(-1)[: 9 * HALF].reshape(9, HALF)

    rows_out = jnp.where(first, jnp.where(masked, 0.0, grad_zero), final)
    ends_here = lax.all_gather(rows_out.astype(low), "heads", axis=0, tiled=True).astype(jnp.float32)
    return (
        ends_here[None], grad_qkv[None], small[6:8][None], grad_out[None], grad_up[None],
        small[8:12].reshape(1, FF), grad_down[None], small[0:2][None], small[2:6][None], ends[0], ends[1:],
    )


def solution(mesh):
    in_specs = (
        P("dp", None), P("dp", None), P("dp"), P(), P(),
        P("section", "dp", None, None), P("section", None, None), P("section", None, "dp"),
        P("section", "dp", None), P("section", None), P("section", None, "dp"),
        P("section", None, None), P("section", None, None), P("dp", None),
    )
    out_specs = (
        P("section", "dp", None), P("section", "dp", None, None), P("section", None, None),
        P("section", None, "dp"), P("section", "dp", None), P("section", None), P("section", None, "dp"),
        P("section", None, None), P("section", None, None), P("section"), P(None, "section"),
    )
    return jax.shard_map(per_device, mesh=mesh, in_specs=in_specs, out_specs=out_specs, check_vma=False)
```

```python
import functools

import jax
import jax.numpy as jnp
from jax import lax
from jax.experimental import pallas as pl
from jax.experimental.pallas import tpu as pltpu
from jax.sharding import PartitionSpec as P

D = 768
HD = 64
FF = 3072
PATCHES = 196
ROWS = 208
GROUPS = 8
HALF = D // 2
HALF_FF = FF // 2
PAIR = 2 * HD
STEPS = 3
CHUNK = HALF_FF // STEPS
FEED = 2 * HALF_FF
ATTN = 4 * HALF
LAYER = FEED + ATTN
JOINED = LAYER + FEED
SIDE = 4
BLOCK = D // SIDE**2
MESH = ("section", "dp", "heads")
SWAP = [(0, 1), (1, 0)]
LIMIT = 48 * 2**20
SCALE = HD ** (-0.5)
epsilon = 1e-06
f32 = jnp.float32
low = jnp.bfloat16


def dot(left, right):
    return jnp.dot(left, right, preferred_element_type=f32)


def dot_t(left, right):
    return lax.dot_general(left, right, (((1,), (1,)), ((), ())), preferred_element_type=f32)


def t_dot(left, right):
    return lax.dot_general(left, right, (((0,), (0,)), ((), ())), preferred_element_type=f32)


def both(own, other):
    return own[...].astype(f32) + other[...].astype(f32)


def column_sum(value):
    return jnp.sum(value.astype(f32), axis=0, keepdims=True)


def stats(value):
    average = jnp.mean(value, axis=-1, keepdims=True)
    centred = value - average
    rate = lax.rsqrt(jnp.mean(centred * centred, axis=-1, keepdims=True) + epsilon)
    return centred * rate, rate


def norm_back(value, gain, grad):
    x, rate = stats(value)
    scaled = grad * gain
    inner = scaled - jnp.mean(scaled, axis=-1, keepdims=True)
    inner = inner - x * jnp.mean(scaled * x, axis=-1, keepdims=True)
    return rate * inner, column_sum(grad * x), column_sum(grad)


def gauss(value):
    return 0.5 + 0.5 * lax.erf(value * 0.7071067811865476), jnp.exp(value * value * -0.5) * 0.3989422804014327


def head_masks():
    left = lax.broadcasted_iota(jnp.int32, (ROWS, PAIR), 1) < HD
    nothing = jnp.zeros((ROWS, PAIR), low)
    return left, (lambda rows: jnp.where(left, rows, nothing), lambda rows: jnp.where(left, nothing, rows))


def raw_scores(key_rows, queries):
    scores = dot_t(key_rows, queries) * SCALE
    return jnp.where(lax.broadcasted_iota(jnp.int32, scores.shape, 0) < PATCHES, scores, -1e30)


def accumulate(step, total, part, low_out):
    @pl.when(step == 0)
    def _():
        total[...] = part

    @pl.when(step > 0)
    def _():
        total[...] += part

    @pl.when(step == STEPS - 1)
    def _():
        low_out[...] = total[...].astype(low)


def slot_rows(slots):
    for i in range(SIDE):
        for j in range(SIDE):
            yield i, j, pl.multiple_of(slots[i] * (SIDE * BLOCK) + slots[SIDE + j] * BLOCK, 16)


def place_rows(slots, pieces, weight, width):
    for i, j, row in slot_rows(slots):
        weight[pl.ds(row, BLOCK), :width] = pieces[j // 2][j % 2, i]
        weight[pl.ds(row, BLOCK), width:] = pieces[2 + i // 2][i % 2, j]


def send_rows(slots, grads, blocks, width):
    for i, j, row in slot_rows(slots):
        blocks[i // 2][i % 2, j] = grads[pl.ds(row, BLOCK), :width]
        blocks[2 + j // 2][j % 2, i] = grads[pl.ds(row, BLOCK), width:]


def attention_kernel(second, *refs):
    if second:
        base, own, other, last_bias, norms, offset, weight, stream_out, *refs = refs
    else:
        slots, base, norms, offset, *refs = refs
        pieces, (weight, *refs) = refs[:SIDE], refs[SIDE:]
    normed_out, packed_out, lse_out, context_out, part_out, total = refs
    step = pl.program_id(0)

    @pl.when(step == 0)
    def _():
        stream = base[...]
        if second:
            stream = (stream + (both(own, other) + last_bias[...])).astype(low).astype(f32)
            stream_out[...] = stream
        normed_out[...] = (stats(stream)[0] * norms[0:1] + norms[2:3]).astype(low)

    if not second:
        place_rows(slots, pieces, weight, 2 * PAIR)
    packed = (dot(normed_out[...], weight[:, : 3 * PAIR]) + offset[...]).astype(low)
    packed_out[...] = packed
    left, choose = head_masks()
    queries, keys, values = (packed[:, k * PAIR : (k + 1) * PAIR] for k in range(3))
    found = []
    for head in range(2):
        scores = raw_scores(keys, choose[head](queries))
        summit = jnp.max(scores, axis=0, keepdims=True)
        raised = jnp.exp(scores - summit)
        whole = jnp.sum(raised, axis=0, keepdims=True)
        lse_out[0, head : head + 1, :] = summit + jnp.log(whole)
        found.append(t_dot((raised * (1.0 / whole)).astype(low), values))
    context = jnp.where(left, found[0], found[1]).astype(low)
    context_out[...] = context
    accumulate(step, total, dot_t(context, weight[:, 3 * PAIR :]), part_out)


def forward_kernel(stream, own, other, norms, bias, weight, middle_out, normed_out, upper_out, part_out, total):
    step = pl.program_id(0)

    @pl.when(step == 0)
    def _():
        middle = stream[...] + (both(own, other) + norms[3:4])
        middle_out[...] = middle
        normed_out[...] = (stats(middle)[0] * norms[1:2] + norms[4:5]).astype(low)

    upper = dot(normed_out[...], weight[:, :CHUNK]) + bias[...]
    upper_out[...] = upper
    hidden = (upper * gauss(upper)[0]).astype(low)
    accumulate(step, total, dot_t(hidden, weight[:, CHUNK:]), part_out)


def turn_kernel(
    branch, stream, own, other, norms, bias, weight,
    grads_out, middle_out, mixed_out, part_out, bias_out, rows_out, normed, mixed, total,
):
    step = pl.program_id(0)

    @pl.when(step == 0)
    def _():
        middle = stream[...] + (both(own, other) + norms[3:4])
        middle_out[...] = middle
        normed[...] = (stats(middle)[0] * norms[1:2] + norms[4:5]).astype(low)
        rows_out[2:3] = column_sum(branch[...])

    rows = branch[...]
    upper = dot(normed[...], weight[:, :CHUNK]) + bias[...]
    share, density = gauss(upper)
    hidden = (upper * share).astype(low)
    grad_upper = (dot(rows, weight[:, CHUNK:]) * (share + upper * density)).astype(low)
    accumulate(step, total, dot_t(grad_upper, weight[:, :CHUNK]), part_out)
    grads_out[:, :CHUNK] = t_dot(normed[...], grad_upper).astype(low)
    grads_out[:, CHUNK:] = t_dot(rows, hidden).astype(low)
    bias_out[...] = column_sum(grad_upper)
    accumulate(step, mixed, dot_t(hidden, weight[:, CHUNK:]), mixed_out)


def backward_kernel(
    grad, own, other, stream, gains, normed, upper, weight, _, grads, part_out, bias_out, rows_out, branch, total
):
    step = pl.program_id(0)

    @pl.when(step == 0)
    def _():
        into, gain, shift = norm_back(stream[...], gains[0:1], both(own, other))
        branch[...] = (grad[...] + into).astype(low)
        rows_out[0:1] = gain
        rows_out[1:2] = shift
        rows_out[2:3] = column_sum(branch[...])

    rows = branch[...]
    upper_now = upper[...]
    share, density = gauss(upper_now)
    hidden = (upper_now * share).astype(low)
    grad_upper = (dot(rows, weight[:, CHUNK:]) * (share + upper_now * density)).astype(low)
    accumulate(step, total, dot_t(grad_upper, weight[:, :CHUNK]), part_out)
    grads[:, :CHUNK] = t_dot(normed[...], grad_upper).astype(low)
    grads[:, CHUNK:] = t_dot(rows, hidden).astype(low)
    bias_out[...] = column_sum(grad_upper)


def attention_back_kernel(second, *refs):
    if not second:
        slots, *refs = refs
    branch, own, other, middle, norms, normed, packed, lse, context, weight, *refs = refs
    if second:
        _, grads, *refs = refs
    else:
        blocks, refs = refs[:SIDE], refs[SIDE:]
    middle_out, part_out, rows_out, packed_out, attn, total, grad_packed, *refs = refs
    if not second:
        (grads,) = refs
    step = pl.program_id(0)

    @pl.when(step == 0)
    def _():
        into, gain, shift = norm_back(middle[...], norms[1:2], both(own, other))
        grad_middle = branch[...].astype(f32) + into
        middle_out[...] = grad_middle
        attn[...] = grad_middle.astype(low)
        rows_out[0:1] = gain
        rows_out[1:2] = shift
        rows_out[2:3] = column_sum(attn[...])

    grad_pair = dot(attn[...], weight[:, 3 * PAIR :]).astype(low)
    left, choose = head_masks()
    queries, keys, values = (packed[:, k * PAIR : (k + 1) * PAIR] for k in range(3))
    found = []
    for head in range(2):
        soft = jnp.exp(raw_scores(keys, choose[head](queries)) - lse[0, head : head + 1, :])
        grad_probs = dot_t(values, choose[head](grad_pair))
        within = jnp.sum(grad_probs * soft, axis=0, keepdims=True)
        grad_scores = (soft * (grad_probs - within)).astype(low)
        found.append((t_dot(grad_scores, keys) * SCALE, dot(grad_scores, queries) * SCALE, dot(soft.astype(low), grad_pair)))
    for k in range(3):
        grad_packed[:, k * PAIR : (k + 1) * PAIR] = jnp.where(left, found[0][k], found[1][k]).astype(low)
    rows = grad_packed[...]
    accumulate(step, total, dot_t(rows, weight[:, : 3 * PAIR]), part_out)
    grads[:, : 3 * PAIR] = t_dot(normed[...], rows).astype(low)
    grads[:, 3 * PAIR :] = t_dot(attn[...], context[...]).astype(low)
    if not second:
        send_rows(slots, grads, blocks, 2 * PAIR)
    packed_out[...] = column_sum(rows)


def last_kernel(
    core, grad_middle, own, other, stream, norms, masked, tag, middle, mixed, mixed_other, last_bias,
    rows_one, sums_one, turn_rows, bias_one, rows_zero, sums_zero, back_rows, bias_zero, rows_out, vectors_out,
):
    into, gain, shift = norm_back(stream[...], norms[0:1], both(own, other))
    grad_zero = grad_middle[...] + into
    hidden = masked[...] > 0.5
    final = middle[...] + (both(mixed, mixed_other) + last_bias[...])
    first = core[0] == 0
    rows_out[...] = jnp.where(first, jnp.where(hidden, 0.0, grad_zero), final).astype(low)
    for at, gain_one, shift_one, attn_rows, feed_rows, sums, bias in (
        (0, gain, shift, rows_zero, back_rows, sums_zero, bias_zero),
        (9, back_rows[0:1], back_rows[1:2], rows_one, turn_rows, sums_one, bias_one),
    ):
        for k, row in enumerate((gain_one, attn_rows[0:1], shift_one, attn_rows[2:3], attn_rows[1:2], feed_rows[2:3])):
            vectors_out[at + k : at + k + 1] = row
        for k in range(STEPS):
            for part in range(2):
                to = part * HALF + k * PAIR
                vectors_out[at + 6 : at + 7, to : to + PAIR] = sums[:, (3 * k + 2 * part) * PAIR : (3 * k + 2 * part + 1) * PAIR]
        for k in range(2):
            vectors_out[at + 7 + k : at + 8 + k] = bias[:, k * D : (k + 1) * D]
    vectors_out[18:19] = column_sum(jnp.where(hidden, grad_zero, 0.0))
    table = column_sum(grad_zero)
    for group in range(GROUPS):
        vectors_out[19 + group : 20 + group] = jnp.where(tag[0] == group, table, 0.0)
    vectors_out[27:32] = jnp.zeros((5, D), f32)


def ends_kernel(order, parts, out):
    for k in range(SIDE):
        out[k * PATCHES : (k + 1) * PATCHES] = parts[order[k]].astype(f32)[:PATCHES]


def shards_kernel(core, qkv, out, up, down, mine_out, sent_out):
    def fill(half, target):
        for k in range(STEPS):
            at = slice(half * HALF_FF + k * CHUNK, half * HALF_FF + (k + 1) * CHUNK)
            target[:, 2 * k * CHUNK : (2 * k + 1) * CHUNK] = up[:, at].astype(low)
            target[:, (2 * k + 1) * CHUNK : (2 * k + 2) * CHUNK] = down[:, at].astype(low)
            at = slice(half * HALF + k * PAIR, half * HALF + (k + 1) * PAIR)
            for part, rows in enumerate((qkv[0, :, at], qkv[1, :, at], qkv[2, :, at], out[:, at])):
                to = FEED + (part // 2) * 2 * HALF + (2 * k + part % 2) * PAIR
                target[:, to : to + PAIR] = rows.astype(low)

    for index in range(2):
        @pl.when(core[0] == index)
        def _():
            fill(index, mine_out)
            fill(1 - index, sent_out)


def grads_kernel(first_half, second_half, qkv_out, out_out, up_out, down_out):
    for h, part in enumerate((first_half, second_half)):
        for k in range(STEPS):
            to = slice(h * HALF_FF + k * CHUNK, h * HALF_FF + (k + 1) * CHUNK)
            up_out[:, to] = part[:, 2 * k * CHUNK : (2 * k + 1) * CHUNK].astype(f32)
            down_out[:, to] = part[:, (2 * k + 1) * CHUNK : (2 * k + 2) * CHUNK].astype(f32)
            to = slice(h * HALF + k * PAIR, h * HALF + (k + 1) * PAIR)
            at = FEED + 4 * k * PAIR
            for c in range(3):
                qkv_out[c, :, to] = part[:, at + c * PAIR : at + (c + 1) * PAIR].astype(f32)
            out_out[:, to] = part[:, at + 3 * PAIR : at + 4 * PAIR].astype(f32)


def whole(array):
    return pl.BlockSpec(array.shape, lambda *_: (0,) * len(array.shape))


def shaped(shape, kind=f32):
    return jax.ShapeDtypeStruct(shape, kind)


def call(kernel, name, operands, outs, specs, flops=0, moved=2**20, grid=STEPS, alias=None, scratch=()):
    def spec(key, array):
        return specs.get(key) or whole(array)

    return pl.pallas_call(
        kernel,
        name=name,
        grid=(grid,),
        in_specs=[spec(("in", k), a) for k, a in enumerate(operands)],
        out_specs=[spec(("out", k), a) for k, a in enumerate(outs)],
        out_shape=outs,
        scratch_shapes=scratch,
        input_output_aliases=alias or {},
        cost_estimate=pl.CostEstimate(flops=flops, bytes_accessed=moved, transcendentals=0),
        compiler_params=pltpu.CompilerParams(vmem_limit_bytes=LIMIT),
    )(*operands)


SMALL = pl.BlockSpec(memory_space=pltpu.SMEM)
LEFT = pl.BlockSpec(memory_space=pl.ANY)


def by_step(shape, start=0):
    return pl.BlockSpec(shape, lambda i: (0,) * (len(shape) - 1) + (start + i,))


FEED_WEIGHT = by_step((D, 2 * CHUNK))
ATTN_WEIGHT = by_step((D, 4 * PAIR))
ATTN_JOINED = by_step((D, 4 * PAIR), 2 * FEED // (4 * PAIR))
FEED_ZERO = by_step((D, 2 * CHUNK), STEPS)
ATTN_PIECE = by_step((2, SIDE, BLOCK, 2 * PAIR))
TRIPLE = by_step((ROWS, 3 * PAIR))
LSE = pl.BlockSpec((1, 8, ROWS), lambda i: (i, 0, 0))
STREAM = shaped((ROWS, D))
STREAM_LOW = shaped((ROWS, D), low)
TOTAL = pltpu.VMEM((ROWS, D), f32)
ATTN_FLOPS = 2 * ROWS * D * ATTN
FEED_FLOPS = 2 * ROWS * D * FEED
HEAD_FLOPS = 2 * ROWS * ROWS * PAIR * 2 * STEPS


def attention_call(layer, entry, norms, offset, weights):
    second = layer == 1
    operands = (*entry, norms, offset, *weights)
    outs = [STREAM_LOW, shaped((ROWS, 3 * HALF), low), shaped((STEPS, 8, ROWS)), shaped((ROWS, HALF), low), STREAM_LOW]
    outs = [STREAM if second else shaped((D, ATTN), low), *outs]
    last = len(operands) - 1
    specs = {("out", 2): TRIPLE, ("out", 3): LSE, ("out", 4): by_step((ROWS, PAIR))}
    if second:
        specs["in", last] = ATTN_JOINED
        specs["in", last - 1] = by_step((1, 3 * PAIR))
    else:
        specs["in", 0] = SMALL
        specs["out", 0] = ATTN_WEIGHT
        specs["in", last - SIDE] = by_step((1, 3 * PAIR))
        for k in range(SIDE):
            specs["in", last - k] = ATTN_PIECE
    return call(
        functools.partial(attention_kernel, second), f"attention_{layer}", operands, outs, specs,
        ATTN_FLOPS + 2 * HEAD_FLOPS, 8 * D * ATTN, scratch=[TOTAL],
    )


def forward_call(stream, part, part_other, norms, bias_up, weight):
    return call(
        forward_kernel, "feed_0", (stream, part, part_other, norms, bias_up, weight),
        [STREAM, STREAM_LOW, shaped((ROWS, HALF_FF)), STREAM_LOW],
        {("in", 4): by_step((1, CHUNK)), ("in", 5): FEED_ZERO, ("out", 2): by_step((ROWS, CHUNK))},
        FEED_FLOPS, 6 * D * FEED, scratch=[TOTAL],
    )


def turn_call(branch, stream, part, part_other, norms, bias_up, weight):
    return call(
        turn_kernel, "feed_1", (branch, stream, part, part_other, norms, bias_up, weight),
        [shaped((D, JOINED), low), STREAM, STREAM_LOW, STREAM_LOW, shaped((1, HALF_FF)), shaped((8, D))],
        {("in", 5): by_step((1, CHUNK)), ("in", 6): FEED_WEIGHT, ("out", 0): FEED_WEIGHT, ("out", 4): by_step((1, CHUNK))},
        3 * FEED_FLOPS, 8 * D * FEED, scratch=[pltpu.VMEM((ROWS, D), low), TOTAL, TOTAL],
    )


def backward_call(entry, normed, upper, weight, grads):
    return call(
        backward_kernel, "feed_back_0", (*entry, normed, upper, weight, grads),
        [shaped((D, JOINED), low), STREAM_LOW, shaped((1, HALF_FF)), shaped((8, D)), STREAM_LOW],
        {
            ("in", 6): by_step((ROWS, CHUNK)), ("in", 7): FEED_ZERO, ("in", 8): LEFT,
            ("out", 0): FEED_ZERO, ("out", 2): by_step((1, CHUNK)),
        },
        2 * FEED_FLOPS, 8 * D * FEED, alias={8: 0}, scratch=[TOTAL],
    )


def attention_back_call(layer, entry, branch, part, part_other, middle, norms, normed, packed, lse, context, weight, grads):
    second = layer == 1
    operands = (*entry, branch, part, part_other, middle, norms, normed, packed, lse, context, weight, *grads)
    outs = [shaped((D, JOINED), low)] if second else [shaped((2, SIDE, BLOCK, 2 * HALF), low)] * SIDE
    skip, count = len(entry), len(outs)
    specs = {
        ("in", skip + 6): TRIPLE, ("in", skip + 7): LSE, ("in", skip + 8): by_step((ROWS, PAIR)),
        ("in", skip + 9): ATTN_JOINED if second else ATTN_WEIGHT, ("out", count + 3): by_step((1, 3 * PAIR)),
    }
    scratch = [pltpu.VMEM((ROWS, D), low), TOTAL, pltpu.VMEM((ROWS, 3 * PAIR), low)]
    if second:
        specs["in", 10], specs["out", 0] = LEFT, ATTN_JOINED
    else:
        specs["in", 0] = SMALL
        for k in range(SIDE):
            specs["out", k] = ATTN_PIECE
        scratch.append(pltpu.VMEM((D, 4 * PAIR), low))
    made = call(
        functools.partial(attention_back_kernel, second), f"attention_back_{layer}", operands,
        [*outs, STREAM, STREAM_LOW, shaped((8, D)), shaped((1, 3 * HALF))], specs,
        2 * ATTN_FLOPS + 5 * HEAD_FLOPS, 8 * D * ATTN, alias={10: 0} if second else None, scratch=scratch,
    )
    return made[:count], made[count:]


def swap(value):
    return lax.ppermute(value, "section", SWAP)


def routes(axis, turn):
    pairs = []
    for place in range(2 * SIDE**3):
        spot = [place // SIDE**3, place // SIDE**2 % SIDE, place // SIDE % SIDE, place % SIDE]
        spot[axis + 1] ^= 1 if spot[0] == turn else 3
        pairs.append((place, ((spot[0] * SIDE + spot[1]) * SIDE + spot[2]) * SIDE + spot[3]))
    return pairs


def trade(value, axis, turn):
    return lax.ppermute(value, MESH, routes(axis, turn))


def add(*values):
    return functools.reduce(jnp.add, (v.astype(f32) for v in values)).astype(low)


def both_of(own, axis, turn):
    return jnp.stack([own, trade(own, axis, turn)])


def gather_first(own, axis):
    pair = both_of(own, axis, 0)
    return jnp.concatenate([pair, trade(pair, axis, 1)])


def gather_second(own, axis):
    pair = both_of(own, axis, 0)
    return pair, trade(pair, axis, 1)


def halves_of(kept, got):
    middle = kept.shape[0] // 2
    return add(kept[:middle], got[:middle]), add(kept[middle:], got[middle:])


def all_sum(value, axis):
    value = value + trade(value, axis, 0)
    return value + trade(value, axis, 1)


tied = lax.optimization_barrier


def per_device(
    patches, mask_flags, image_tags, mask_token, group_table, qkv_weight, query_value_bias, out_weight,
    up_weight, hidden_bias, down_weight, norm_gains, norm_biases, cotangent,
):
    place = lax.axis_index("heads")
    core = lax.axis_index("section")
    first = core == 0

    rows = qkv_weight.shape[1]
    mine, other = call(
        shards_kernel, "shards",
        (core.reshape(1), qkv_weight[0].transpose(1, 0, 2), out_weight[0].T, up_weight[0], down_weight[0].T),
        [shaped((rows, LAYER), low)] * 2, {("in", 0): SMALL}, grid=1,
    )
    other = swap(other)
    zero, one = jnp.where(first, mine, other), jnp.where(first, other, mine)

    def by_pair(wide):
        return [wide[:, s * 2 * HALF + k * 2 * PAIR : s * 2 * HALF + (k + 1) * 2 * PAIR] for k in range(STEPS) for s in (0, 1)]

    shard = jnp.concatenate([one[:, :FEED], zero[:, :FEED], *by_pair(one[:, FEED:])], axis=1)
    weights = lax.all_gather(shard, "dp", axis=0, tiled=True)
    pieces = gather_first(zero[:, FEED : FEED + 2 * HALF], 0), gather_first(zero[:, FEED + 2 * HALF :], 1)
    pieces = (*gather_second(pieces[0], 1), *gather_second(pieces[1], 0))
    later = (patches, mask_flags, image_tags, mask_token, group_table, cotangent, norm_gains, norm_biases, query_value_bias, hidden_bias)
    later, _ = tied((later, shard))
    patches, mask_flags, image_tags, mask_token, group_table, cotangent, norm_gains, norm_biases, query_value_bias, hidden_bias = later

    x, y = lax.axis_index("dp") // SIDE, lax.axis_index("dp") % SIDE
    flips = jnp.where(first, jnp.array([0, 1, 3, 2], jnp.int32), jnp.array([0, 3, 1, 2], jnp.int32))
    slots = jnp.concatenate([x ^ flips, y ^ flips])
    order = jnp.argmax((place ^ flips)[None, :] == jnp.arange(SIDE, dtype=jnp.int32)[:, None], axis=1).astype(jnp.int32)

    def half_of(vector):
        return jnp.where(first, vector[..., : vector.shape[-1] // 2], vector[..., vector.shape[-1] // 2 :])

    vectors = lax.all_gather(
        jnp.concatenate([norm_gains[0], norm_biases[0], query_value_bias[0], hidden_bias[0].reshape(4, D)]),
        "section", axis=0,
    )
    norms, offsets, bias_ups = [], [], []
    for layer in range(2):
        v = vectors[layer]
        norms.append(jnp.pad(v[:6], ((0, 2), (0, 0))))
        query, value = half_of(v[6:8]).reshape(2, STEPS, PAIR)
        offsets.append(jnp.stack([query, jnp.zeros_like(query), value], axis=1).reshape(1, 3 * HALF))
        bias_ups.append(half_of(v[8:12].reshape(1, FF)))

    def own(rows_of):
        return lax.dynamic_slice_in_dim(rows_of, place * PATCHES, PATCHES, 0)

    def padded(value):
        return jnp.pad(value, ((0, ROWS - PATCHES), (0, 0)))

    masked = lax.dynamic_slice_in_dim(mask_flags, place, 1, 0).reshape(PATCHES, 1).astype(f32)
    tag = lax.dynamic_slice_in_dim(image_tags, place, 1, 0)
    onehot = (tag[:, None] == jnp.arange(GROUPS, dtype=jnp.int32)[None, :]).astype(f32)
    image_row = jnp.sum(onehot.T * group_table, axis=0, keepdims=True)
    stream_zero = padded(jnp.where(masked > 0, mask_token[None, :], own(patches).astype(f32)) + image_row)
    seed, masked = padded(own(cotangent)), padded(masked)

    attn_zero, normed, packed, lse, context, part = attention_call(0, (slots, stream_zero), norms[0], offsets[0], pieces)
    middle, normed_two, upper, mixed = forward_call(stream_zero, part, swap(part), norms[0], bias_ups[0], weights)
    kept = (middle, norms[0], normed, packed, lse, context, attn_zero)
    stream_one, normed, packed, lse, context, part = attention_call(
        1, (middle, mixed, swap(mixed), norms[0][5:6]), norms[1], offsets[1], [weights]
    )
    grads, middle, mixed, part, bias_one, turn_rows = turn_call(
        seed, stream_one, part, swap(part), norms[1], bias_ups[1], weights
    )
    (grads,), (grad_middle, part, rows_one, sums_one) = attention_back_call(
        1, (), seed, part, swap(part), middle, norms[1], normed, packed, lse, context, weights, [grads]
    )
    grads, part, bias_zero, back_rows, branch = backward_call(
        (grad_middle, part, swap(part), stream_one, norms[1]), normed_two, upper, weights, grads
    )
    joined = lax.psum_scatter(grads, "dp", scatter_dimension=0, tiled=True)
    (zero, sent, zero_too, sent_too), (grad_middle, part, rows_zero, sums_zero) = attention_back_call(
        0, (slots,), branch, part, swap(part), *kept, []
    )
    rows_out, small = call(
        last_kernel, "last",
        (
            core.reshape(1), grad_middle, part, swap(part), stream_zero, norms[0], masked, tag, middle, mixed, swap(mixed),
            norms[1][5:6], rows_one, sums_one, turn_rows, bias_one, rows_zero, sums_zero, back_rows, bias_zero,
        ),
        [STREAM_LOW, shaped((32, D))], {("in", 0): SMALL, ("in", 7): SMALL}, grid=1,
    )

    got, got_too = trade(sent, 0, 1), trade(sent_too, 1, 1)
    (zero, sent), (zero_too, sent_too) = halves_of(zero, got), halves_of(zero_too, got_too)
    got, got_too = trade(sent, 0, 0), trade(sent_too, 1, 0)
    (zero, sent), (zero_too, sent_too) = halves_of(zero[0], got[0]), halves_of(zero_too[0], got_too[0])
    got, got_too = trade(sent, 1, 1), trade(sent_too, 0, 1)
    (zero, sent), (zero_too, sent_too) = halves_of(zero, got), halves_of(zero_too, got_too)
    got, got_too = trade(sent, 1, 0), trade(sent_too, 0, 0)
    attn_sum = jnp.concatenate(by_pair(jnp.concatenate([add(zero[0], got[0]), add(zero_too[0], got_too[0])], axis=1)), axis=1)

    def z_sum(value):
        value = add(value, trade(value, 2, 0))
        return add(value, trade(value, 2, 1))

    attn_sum = z_sum(attn_sum)
    for axis in range(3):
        small = all_sum(small, axis)
    ends = both_of(rows_out, 2, 0)
    ends = jnp.concatenate([ends, trade(ends, 2, 1)])
    (ends_here,) = call(
        ends_kernel, "ends", (order, ends), [shaped((SIDE * PATCHES, D))], {("in", 0): SMALL}, grid=1
    )
    small_mine = jnp.where(first, small[:9], small[9:18])
    half_other = swap(jnp.where(first, small[15:18], small[6:9]))
    half_mine = small_mine[6:9]
    half_both = jnp.where(first, half_mine, half_other), jnp.where(first, half_other, half_mine)
    grad_qv = jnp.concatenate([h[0].reshape(2, HALF) for h in half_both], axis=1)
    grad_hidden = jnp.concatenate([h[1:].reshape(1, HALF_FF) for h in half_both], axis=1)
    ends_grads = half_of(small[18:27])

    joined, attn_sum, ends_here, small_mine, grad_qv, grad_hidden, ends_grads = tied(
        (joined, attn_sum, ends_here, small_mine, grad_qv, grad_hidden, ends_grads)
    )
    joined = z_sum(joined)
    zero = jnp.concatenate([joined[:, FEED : 2 * FEED], attn_sum], axis=1)
    one = jnp.concatenate([joined[:, :FEED], joined[:, 2 * FEED :]], axis=1)
    mine = jnp.where(first, zero, one)
    other = swap(jnp.where(first, one, zero))
    grad_qkv, grad_out, grad_up, grad_down = call(
        grads_kernel, "grads", (jnp.where(first, mine, other), jnp.where(first, other, mine)),
        [shaped((3, rows, D)), shaped((rows, D)), shaped((rows, FF)), shaped((rows, FF))], {}, grid=1,
    )
    return (
        ends_here[None], grad_qkv.transpose(1, 0, 2)[None], grad_qv[None], grad_out.T[None], grad_up[None], grad_hidden, grad_down.T[None],
        small_mine[None, 0:2], small_mine[None, 2:6], ends_grads[0], ends_grads[1:],
    )


def solution(mesh):
    in_specs = (
        P("dp", None), P("dp", None), P("dp"), P(), P(),
        P("section", "dp", None, None), P("section", None, None), P("section", None, "dp"),
        P("section", "dp", None), P("section", None), P("section", None, "dp"),
        P("section", None, None), P("section", None, None), P("dp", None),
    )
    out_specs = (
        P("section", "dp", None), P("section", "dp", None, None), P("section", None, None),
        P("section", None, "dp"), P("section", "dp", None), P("section", None), P("section", None, "dp"),
        P("section", None, None), P("section", None, None), P("section"), P(None, "section"),
    )
    return jax.shard_map(per_device, mesh=mesh, in_specs=in_specs, out_specs=out_specs, check_vma=False)
```

```python
import functools

import jax
import jax.numpy as jnp
from jax import lax
from jax.experimental import pallas as pl
from jax.experimental.pallas import tpu as pltpu
from jax.sharding import PartitionSpec as P

D = 768
HD = 64
FF = 3072
PATCHES = 196
ROWS = 208
GROUPS = 8
HALF = D // 2
HALF_FF = FF // 2
PAIR = 2 * HD
STEPS = 3
CHUNK = HALF_FF // STEPS
FEED = 2 * HALF_FF
ATTN = 4 * HALF
LAYER = FEED + ATTN
JOINED = LAYER + FEED
SIDE = 4
BLOCK = D // SIDE**2
MESH = ("section", "dp", "heads")
SWAP = [(0, 1), (1, 0)]
LIMIT = 48 * 2**20
SCALE = HD ** (-0.5)
epsilon = 1e-06
f32 = jnp.float32
low = jnp.bfloat16


def dot(left, right):
    return jnp.dot(left, right, preferred_element_type=f32)


def dot_t(left, right):
    return lax.dot_general(left, right, (((1,), (1,)), ((), ())), preferred_element_type=f32)


def t_dot(left, right):
    return lax.dot_general(left, right, (((0,), (0,)), ((), ())), preferred_element_type=f32)


def both(own, other):
    return own[...].astype(f32) + other[...].astype(f32)


def column_sum(value):
    return jnp.sum(value.astype(f32), axis=0, keepdims=True)


def stats(value):
    average = jnp.mean(value, axis=-1, keepdims=True)
    centred = value - average
    rate = lax.rsqrt(jnp.mean(centred * centred, axis=-1, keepdims=True) + epsilon)
    return centred * rate, rate


def norm_back(value, gain, grad):
    x, rate = stats(value)
    scaled = grad * gain
    inner = scaled - jnp.mean(scaled, axis=-1, keepdims=True)
    inner = inner - x * jnp.mean(scaled * x, axis=-1, keepdims=True)
    return rate * inner, column_sum(grad * x), column_sum(grad)


def gauss(value):
    return 0.5 + 0.5 * lax.erf(value * 0.7071067811865476), jnp.exp(value * value * -0.5) * 0.3989422804014327


def head_masks():
    left = lax.broadcasted_iota(jnp.int32, (ROWS, PAIR), 1) < HD
    nothing = jnp.zeros((ROWS, PAIR), low)
    return left, (lambda rows: jnp.where(left, rows, nothing), lambda rows: jnp.where(left, nothing, rows))


def raw_scores(key_rows, queries):
    scores = dot_t(key_rows, queries) * SCALE
    return jnp.where(lax.broadcasted_iota(jnp.int32, scores.shape, 0) < PATCHES, scores, -1e30)


def accumulate(step, total, part, low_out):
    @pl.when(step == 0)
    def _():
        total[...] = part

    @pl.when(step > 0)
    def _():
        total[...] += part

    @pl.when(step == STEPS - 1)
    def _():
        low_out[...] = total[...].astype(low)


def slot_rows(slots):
    for i in range(SIDE):
        for j in range(SIDE):
            yield i, j, pl.multiple_of(slots[i] * (SIDE * BLOCK) + slots[SIDE + j] * BLOCK, 16)


def place_rows(slots, pieces, weight, width):
    for i, j, row in slot_rows(slots):
        weight[pl.ds(row, BLOCK), :width] = pieces[j // 2][j % 2, i]
        weight[pl.ds(row, BLOCK), width:] = pieces[2 + i // 2][i % 2, j]


def send_rows(slots, grads, blocks, width):
    for i, j, row in slot_rows(slots):
        blocks[i // 2][i % 2, j] = grads[pl.ds(row, BLOCK), :width]
        blocks[2 + j // 2][j % 2, i] = grads[pl.ds(row, BLOCK), width:]


def column_copies(whole, parts, sems, start, size, outwards=False):
    copies = []
    for k in range(STEPS):
        ends = whole.at[:, pl.ds(start + k * size, size)], parts.at[k]
        copies.append(pltpu.make_async_copy(*(reversed(ends) if outwards else ends), sems.at[k]))
    return copies


def pair_forward(packed, write_lse):
    left, choose = head_masks()
    queries, keys, values = (packed[:, k * PAIR : (k + 1) * PAIR] for k in range(3))
    found = []
    for head in range(2):
        scores = raw_scores(keys, choose[head](queries))
        summit = jnp.max(scores, axis=0, keepdims=True)
        raised = jnp.exp(scores - summit)
        whole = jnp.sum(raised, axis=0, keepdims=True)
        write_lse(head, summit + jnp.log(whole))
        found.append(t_dot((raised * (1.0 / whole)).astype(low), values))
    return jnp.where(left, found[0], found[1]).astype(low)


def pair_backward(packed, lse, grad_pair, grad_packed):
    left, choose = head_masks()
    queries, keys, values = (packed[:, k * PAIR : (k + 1) * PAIR] for k in range(3))
    found = []
    for head in range(2):
        soft = jnp.exp(raw_scores(keys, choose[head](queries)) - lse[head : head + 1, :])
        grad_probs = dot_t(values, choose[head](grad_pair))
        within = jnp.sum(grad_probs * soft, axis=0, keepdims=True)
        grad_scores = (soft * (grad_probs - within)).astype(low)
        found.append((t_dot(grad_scores, keys) * SCALE, dot(grad_scores, queries) * SCALE, dot(soft.astype(low), grad_pair)))
    for k in range(3):
        grad_packed[:, k * PAIR : (k + 1) * PAIR] = jnp.where(left, found[0][k], found[1][k]).astype(low)
    return grad_packed[...]


def attention_zero_kernel(slots, base, norms, offset, *refs):
    pieces, (weight, normed_out, packed_out, lse_out, context_out, part_out, total) = refs[:SIDE], refs[SIDE:]
    step = pl.program_id(0)

    @pl.when(step == 0)
    def _():
        normed_out[...] = (stats(base[...])[0] * norms[0:1] + norms[2:3]).astype(low)

    place_rows(slots, pieces, weight, 2 * PAIR)
    packed = (dot(normed_out[...], weight[:, : 3 * PAIR]) + offset[...]).astype(low)
    packed_out[...] = packed

    def write_lse(head, row):
        lse_out[0, head : head + 1, :] = row

    context = pair_forward(packed, write_lse)
    context_out[...] = context
    accumulate(step, total, dot_t(context, weight[:, 3 * PAIR :]), part_out)


def attention_one_kernel(
    base, own, other, last_bias, norms, offset, weights,
    stream_out, normed_out, packed_out, lse_out, context_out, part_out, weight, sems,
):
    copies = column_copies(weights, weight, sems, 2 * FEED, 4 * PAIR)
    for copy in copies:
        copy.start()
    stream = (base[...] + (both(own, other) + last_bias[...])).astype(low).astype(f32)
    stream_out[...] = stream
    normed = (stats(stream)[0] * norms[0:1] + norms[2:3]).astype(low)
    normed_out[...] = normed
    total = 0.0
    for k in range(STEPS):
        copies[k].wait()
        at = slice(k * 3 * PAIR, (k + 1) * 3 * PAIR)
        packed = (dot(normed, weight[k, :, : 3 * PAIR]) + offset[:, at]).astype(low)
        packed_out[:, at] = packed

        def write_lse(head, row):
            lse_out[k, head : head + 1, :] = row

        context = pair_forward(packed, write_lse)
        context_out[:, k * PAIR : (k + 1) * PAIR] = context
        total = total + dot_t(context, weight[k, :, 3 * PAIR :])
    part_out[...] = total.astype(low)


def forward_kernel(
    stream, own, other, norms, bias, weights, middle_out, normed_out, upper_out, part_out, weight, kept, sems, out_sems
):
    copies = column_copies(weights, weight, sems, FEED, 2 * CHUNK)
    for copy in copies:
        copy.start()
    leaving = column_copies(upper_out, kept, out_sems, 0, CHUNK, True)
    middle = stream[...] + (both(own, other) + norms[3:4])
    middle_out[...] = middle
    normed = (stats(middle)[0] * norms[1:2] + norms[4:5]).astype(low)
    normed_out[...] = normed
    total = 0.0
    for k in range(STEPS):
        copies[k].wait()
        upper = dot(normed, weight[k, :, :CHUNK]) + bias[:, k * CHUNK : (k + 1) * CHUNK]
        kept[k] = upper
        leaving[k].start()
        hidden = (upper * gauss(upper)[0]).astype(low)
        total = total + dot_t(hidden, weight[k, :, CHUNK:])
    part_out[...] = total.astype(low)
    for copy in leaving:
        copy.wait()


def turn_kernel(
    branch, stream, own, other, norms, bias, weights,
    grads_out, middle_out, mixed_out, part_out, bias_out, rows_out, weight, grads, sems, out_sems,
):
    copies = column_copies(weights, weight, sems, 0, 2 * CHUNK)
    for copy in copies:
        copy.start()
    leaving = column_copies(grads_out, grads, out_sems, 0, 2 * CHUNK, True)
    middle = stream[...] + (both(own, other) + norms[3:4])
    middle_out[...] = middle
    normed = (stats(middle)[0] * norms[1:2] + norms[4:5]).astype(low)
    rows = branch[...]
    rows_out[2:3] = column_sum(rows)
    total = mixed = 0.0
    for k in range(STEPS):
        at = slice(k * CHUNK, (k + 1) * CHUNK)
        copies[k].wait()
        upper = dot(normed, weight[k, :, :CHUNK]) + bias[:, at]
        share, density = gauss(upper)
        hidden = (upper * share).astype(low)
        grad_upper = (dot(rows, weight[k, :, CHUNK:]) * (share + upper * density)).astype(low)
        total = total + dot_t(grad_upper, weight[k, :, :CHUNK])
        grads[k, :, :CHUNK] = t_dot(normed, grad_upper).astype(low)
        grads[k, :, CHUNK:] = t_dot(rows, hidden).astype(low)
        leaving[k].start()
        bias_out[:, at] = column_sum(grad_upper)
        mixed = mixed + dot_t(hidden, weight[k, :, CHUNK:])
    part_out[...] = total.astype(low)
    mixed_out[...] = mixed.astype(low)
    for copy in leaving:
        copy.wait()


def backward_kernel(
    grad, own, other, stream, gains, normed_in, uppers, weights, _,
    grads_out, part_out, bias_out, rows_out, branch, weight, upper, grads, sems, upper_sems, out_sems,
):
    copies = column_copies(weights, weight, sems, FEED, 2 * CHUNK)
    entering = column_copies(uppers, upper, upper_sems, 0, CHUNK)
    for pair in zip(copies, entering):
        for copy in pair:
            copy.start()
    leaving = column_copies(grads_out, grads, out_sems, FEED, 2 * CHUNK, True)
    into, gain, shift = norm_back(stream[...], gains[0:1], both(own, other))
    rows = (grad[...] + into).astype(low)
    branch[...] = rows
    rows_out[0:1] = gain
    rows_out[1:2] = shift
    rows_out[2:3] = column_sum(rows)
    normed = normed_in[...]
    total = 0.0
    for k in range(STEPS):
        entering[k].wait()
        copies[k].wait()
        upper_now = upper[k]
        share, density = gauss(upper_now)
        hidden = (upper_now * share).astype(low)
        grad_upper = (dot(rows, weight[k, :, CHUNK:]) * (share + upper_now * density)).astype(low)
        total = total + dot_t(grad_upper, weight[k, :, :CHUNK])
        grads[k, :, :CHUNK] = t_dot(normed, grad_upper).astype(low)
        grads[k, :, CHUNK:] = t_dot(rows, hidden).astype(low)
        leaving[k].start()
        bias_out[:, k * CHUNK : (k + 1) * CHUNK] = column_sum(grad_upper)
    part_out[...] = total.astype(low)
    for copy in leaving:
        copy.wait()


def attention_back_one_kernel(
    branch, own, other, middle, norms, normed_in, packed, lse, context, weights, _,
    grads_out, middle_out, part_out, rows_out, packed_out, weight, grads, grad_packed, sems, out_sems,
):
    copies = column_copies(weights, weight, sems, 2 * FEED, 4 * PAIR)
    for copy in copies:
        copy.start()
    leaving = column_copies(grads_out, grads, out_sems, 2 * FEED, 4 * PAIR, True)
    into, gain, shift = norm_back(middle[...], norms[1:2], both(own, other))
    grad_middle = branch[...].astype(f32) + into
    middle_out[...] = grad_middle
    attn = grad_middle.astype(low)
    rows_out[0:1] = gain
    rows_out[1:2] = shift
    rows_out[2:3] = column_sum(attn)
    normed = normed_in[...]
    total = 0.0
    for k in range(STEPS):
        at = slice(k * 3 * PAIR, (k + 1) * 3 * PAIR)
        copies[k].wait()
        grad_pair = dot(attn, weight[k, :, 3 * PAIR :]).astype(low)
        rows = pair_backward(packed[:, at], lse[k], grad_pair, grad_packed)
        total = total + dot_t(rows, weight[k, :, : 3 * PAIR])
        grads[k, :, : 3 * PAIR] = t_dot(normed, rows).astype(low)
        grads[k, :, 3 * PAIR :] = t_dot(attn, context[:, k * PAIR : (k + 1) * PAIR]).astype(low)
        leaving[k].start()
        packed_out[:, at] = column_sum(rows)
    part_out[...] = total.astype(low)
    for copy in leaving:
        copy.wait()


def attention_back_zero_kernel(
    slots, branch, own, other, middle, norms, normed, packed, lse, context, weight, *refs
):
    blocks, refs = refs[:SIDE], refs[SIDE:]
    middle_out, part_out, rows_out, packed_out, attn, total, grad_packed, grads = refs
    step = pl.program_id(0)

    @pl.when(step == 0)
    def _():
        into, gain, shift = norm_back(middle[...], norms[1:2], both(own, other))
        grad_middle = branch[...].astype(f32) + into
        middle_out[...] = grad_middle
        attn[...] = grad_middle.astype(low)
        rows_out[0:1] = gain
        rows_out[1:2] = shift
        rows_out[2:3] = column_sum(attn[...])

    grad_pair = dot(attn[...], weight[:, 3 * PAIR :]).astype(low)
    rows = pair_backward(packed[...], lse[0], grad_pair, grad_packed)
    accumulate(step, total, dot_t(rows, weight[:, : 3 * PAIR]), part_out)
    grads[:, : 3 * PAIR] = t_dot(normed[...], rows).astype(low)
    grads[:, 3 * PAIR :] = t_dot(attn[...], context[...]).astype(low)
    send_rows(slots, grads, blocks, 2 * PAIR)
    packed_out[...] = column_sum(rows)


def last_kernel(
    core, grad_middle, own, other, stream, norms, masked, tag, middle, mixed, mixed_other, last_bias,
    rows_one, sums_one, turn_rows, bias_one, rows_zero, sums_zero, back_rows, bias_zero, rows_out, vectors_low_out, vectors_out,
):
    into, gain, shift = norm_back(stream[...], norms[0:1], both(own, other))
    grad_zero = grad_middle[...] + into
    hidden = masked[...] > 0.5
    final = middle[...] + (both(mixed, mixed_other) + last_bias[...])
    first = core[0] == 0
    rows_out[...] = jnp.where(first, jnp.where(hidden, 0.0, grad_zero), final).astype(low)
    for at, gain_one, shift_one, attn_rows, feed_rows, sums, bias in (
        (0, gain, shift, rows_zero, back_rows, sums_zero, bias_zero),
        (9, back_rows[0:1], back_rows[1:2], rows_one, turn_rows, sums_one, bias_one),
    ):
        for k, row in enumerate((gain_one, attn_rows[0:1], shift_one, attn_rows[2:3], attn_rows[1:2], feed_rows[2:3])):
            vectors_out[at + k : at + k + 1] = row
        for k in range(STEPS):
            for part in range(2):
                to = part * HALF + k * PAIR
                vectors_out[at + 6 : at + 7, to : to + PAIR] = sums[:, (3 * k + 2 * part) * PAIR : (3 * k + 2 * part + 1) * PAIR]
        for k in range(2):
            vectors_out[at + 7 + k : at + 8 + k] = bias[:, k * D : (k + 1) * D]
    vectors_out[18:19] = column_sum(jnp.where(hidden, grad_zero, 0.0))
    table = column_sum(grad_zero)
    for group in range(GROUPS):
        vectors_out[19 + group : 20 + group] = jnp.where(tag[0] == group, table, 0.0)
    vectors_out[27:32] = jnp.zeros((5, D), f32)
    vectors_low_out[...] = jnp.zeros((BLOCK, 2 * HALF), low)
    vectors_low_out[0:32, 0:D] = vectors_out[...].astype(low)


def ends_kernel(order, parts, out):
    for k in range(SIDE):
        out[k * PATCHES : (k + 1) * PATCHES] = parts[order[k]].astype(f32)[:PATCHES]


def shards_kernel(core, qkv, out, up, down, mine_out, sent_out):
    def fill(half, target):
        for k in range(STEPS):
            at = slice(half * HALF_FF + k * CHUNK, half * HALF_FF + (k + 1) * CHUNK)
            target[:, 2 * k * CHUNK : (2 * k + 1) * CHUNK] = up[:, at].astype(low)
            target[:, (2 * k + 1) * CHUNK : (2 * k + 2) * CHUNK] = down[:, at].astype(low)
            at = slice(half * HALF + k * PAIR, half * HALF + (k + 1) * PAIR)
            for part, rows in enumerate((qkv[0, :, at], qkv[1, :, at], qkv[2, :, at], out[:, at])):
                to = FEED + (part // 2) * 2 * HALF + (2 * k + part % 2) * PAIR
                target[:, to : to + PAIR] = rows.astype(low)

    for index in range(2):
        @pl.when(core[0] == index)
        def _():
            fill(index, mine_out)
            fill(1 - index, sent_out)


def grads_kernel(
    core, first_half, second_half,
    qkv_out, out_out, up_out, down_out, qv_out, hidden_out, gains_out, biases_out, token_out, table_out,
):
    shared = first_half[:, LAYER:].astype(f32)
    for h, half in enumerate((first_half, second_half)):
        for k in range(STEPS):
            to = slice(h * HALF_FF + k * CHUNK, h * HALF_FF + (k + 1) * CHUNK)
            up_out[:, to] = half[:, 2 * k * CHUNK : (2 * k + 1) * CHUNK].astype(f32)
            down_out[:, to] = half[:, (2 * k + 1) * CHUNK : (2 * k + 2) * CHUNK].astype(f32)
            to = slice(h * HALF + k * PAIR, h * HALF + (k + 1) * PAIR)
            at = FEED + 4 * k * PAIR
            for c in range(3):
                qkv_out[c, :, to] = half[:, at + c * PAIR : at + (c + 1) * PAIR].astype(f32)
            out_out[:, to] = half[:, at + 3 * PAIR : at + 4 * PAIR].astype(f32)

    for index in range(2):
        @pl.when(core[0] == index)
        def _():
            at = 9 * index
            gains_out[...] = shared[at : at + 2]
            biases_out[...] = shared[at + 2 : at + 6]
            token_out[...] = shared[18:19, index * HALF : (index + 1) * HALF]
            table_out[...] = shared[19 : 19 + GROUPS, index * HALF : (index + 1) * HALF]
            for h, half in enumerate((first_half, second_half)):
                rows = half[:, LAYER:].astype(f32)
                for k in range(2):
                    qv_out[k : k + 1, h * HALF : (h + 1) * HALF] = rows[at + 6 : at + 7, k * HALF : (k + 1) * HALF]
                    hidden_out[:, h * HALF_FF + k * D : h * HALF_FF + (k + 1) * D] = rows[at + 7 + k : at + 8 + k]


def whole(array):
    return pl.BlockSpec(array.shape, lambda *_: (0,) * len(array.shape))


def shaped(shape, kind=f32):
    return jax.ShapeDtypeStruct(shape, kind)


def call(kernel, name, operands, outs, specs, micros, grid=STEPS, alias=None, scratch=(), limit=LIMIT):
    def spec(key, array):
        return specs.get(key) or whole(array)

    return pl.pallas_call(
        kernel,
        name=name,
        grid=(grid,),
        in_specs=[spec(("in", k), a) for k, a in enumerate(operands)],
        out_specs=[spec(("out", k), a) for k, a in enumerate(outs)],
        out_shape=outs,
        scratch_shapes=scratch,
        input_output_aliases=alias or {},
        cost_estimate=pl.CostEstimate(flops=0, bytes_accessed=int(micros * 3.6e6), transcendentals=0),
        compiler_params=pltpu.CompilerParams(vmem_limit_bytes=limit),
    )(*operands)


SMALL = pl.BlockSpec(memory_space=pltpu.SMEM)
LEFT = pl.BlockSpec(memory_space=pl.ANY)


def by_step(shape):
    return pl.BlockSpec(shape, lambda i: (0,) * (len(shape) - 1) + (i,))


ATTN_WEIGHT = by_step((D, 4 * PAIR))
ATTN_PIECE = by_step((2, SIDE, BLOCK, 2 * PAIR))
TRIPLE = by_step((ROWS, 3 * PAIR))
LSE = pl.BlockSpec((1, 8, ROWS), lambda i: (i, 0, 0))
STREAM = shaped((ROWS, D))
STREAM_LOW = shaped((ROWS, D), low)
TOTAL = pltpu.VMEM((ROWS, D), f32)


DMA = pltpu.SemaphoreType.DMA((STEPS,))
FEED_PARTS = pltpu.VMEM((STEPS, D, 2 * CHUNK), low)
ATTN_PARTS = pltpu.VMEM((STEPS, D, 4 * PAIR), low)
UPPER_PARTS = pltpu.VMEM((STEPS, ROWS, CHUNK), f32)
ATTN_KEPT = [STREAM_LOW, shaped((ROWS, 3 * HALF), low), shaped((STEPS, 8, ROWS)), shaped((ROWS, HALF), low), STREAM_LOW]
JOINED_GRADS = shaped((D, JOINED), low)


def attention_zero_call(slots, stream, norms, offset, pieces):
    operands = (slots, stream, norms, offset, *pieces)
    specs = {
        ("in", 0): SMALL, ("in", 3): by_step((1, 3 * PAIR)), ("out", 0): ATTN_WEIGHT, ("out", 2): TRIPLE, ("out", 3): LSE,
        ("out", 4): by_step((ROWS, PAIR)), **{("in", 4 + k): ATTN_PIECE for k in range(SIDE)},
    }
    return call(
        attention_zero_kernel, "attention_0", operands, [shaped((D, ATTN), low), *ATTN_KEPT], specs, 5, scratch=[TOTAL]
    )


def attention_one_call(base, own, other, last_bias, norms, offset, weights):
    return call(
        attention_one_kernel, "attention_1", (base, own, other, last_bias, norms, offset, weights), [STREAM, *ATTN_KEPT],
        {("in", 6): LEFT}, 4, grid=1, scratch=[ATTN_PARTS, DMA],
    )


def forward_call(stream, part, part_other, norms, bias_up, weights):
    return call(
        forward_kernel, "feed_0", (stream, part, part_other, norms, bias_up, weights),
        [STREAM, STREAM_LOW, shaped((ROWS, HALF_FF)), STREAM_LOW], {("in", 5): LEFT, ("out", 2): LEFT}, 4, grid=1,
        scratch=[FEED_PARTS, UPPER_PARTS, DMA, DMA],
    )


def turn_call(branch, stream, part, part_other, norms, bias_up, weights):
    return call(
        turn_kernel, "feed_1", (branch, stream, part, part_other, norms, bias_up, weights),
        [JOINED_GRADS, STREAM, STREAM_LOW, STREAM_LOW, shaped((1, HALF_FF)), shaped((8, D))],
        {("in", 6): LEFT, ("out", 0): LEFT}, 7, grid=1, scratch=[FEED_PARTS, FEED_PARTS, DMA, DMA],
    )


def backward_call(entry, normed, upper, weights, grads):
    return call(
        backward_kernel, "feed_back_0", (*entry, normed, upper, weights, grads),
        [JOINED_GRADS, STREAM_LOW, shaped((1, HALF_FF)), shaped((8, D)), STREAM_LOW],
        {("in", 6): LEFT, ("in", 7): LEFT, ("in", 8): LEFT, ("out", 0): LEFT}, 6, grid=1, alias={8: 0},
        scratch=[FEED_PARTS, UPPER_PARTS, FEED_PARTS, DMA, DMA, DMA],
    )


def attention_back_one_call(branch, part, part_other, middle, norms, normed, packed, lse, context, weights, grads):
    return call(
        attention_back_one_kernel, "attention_back_1",
        (branch, part, part_other, middle, norms, normed, packed, lse, context, weights, grads),
        [JOINED_GRADS, STREAM, STREAM_LOW, shaped((8, D)), shaped((1, 3 * HALF))],
        {("in", 9): LEFT, ("in", 10): LEFT, ("out", 0): LEFT}, 7, grid=1, alias={10: 0},
        scratch=[ATTN_PARTS, ATTN_PARTS, pltpu.VMEM((ROWS, 3 * PAIR), low), DMA, DMA],
    )


def attention_back_zero_call(slots, branch, part, part_other, middle, norms, normed, packed, lse, context, weight):
    specs = {
        ("in", 0): SMALL, ("in", 7): TRIPLE, ("in", 8): LSE, ("in", 9): by_step((ROWS, PAIR)), ("in", 10): ATTN_WEIGHT,
        ("out", SIDE + 3): by_step((1, 3 * PAIR)), **{("out", k): ATTN_PIECE for k in range(SIDE)},
    }
    made = call(
        attention_back_zero_kernel, "attention_back_0",
        (slots, branch, part, part_other, middle, norms, normed, packed, lse, context, weight),
        [*[shaped((2, SIDE, BLOCK, 2 * HALF), low)] * SIDE, STREAM, STREAM_LOW, shaped((8, D)), shaped((1, 3 * HALF))],
        specs, 9,
        scratch=[pltpu.VMEM((ROWS, D), low), TOTAL, pltpu.VMEM((ROWS, 3 * PAIR), low), pltpu.VMEM((D, 4 * PAIR), low)],
    )
    return made[:SIDE], made[SIDE:]


def swap(value):
    return lax.ppermute(value, "section", SWAP)


def routes(axis, turn):
    pairs = []
    for place in range(2 * SIDE**3):
        spot = [place // SIDE**3, place // SIDE**2 % SIDE, place // SIDE % SIDE, place % SIDE]
        spot[axis + 1] ^= 1 if spot[0] == turn else 3
        pairs.append((place, ((spot[0] * SIDE + spot[1]) * SIDE + spot[2]) * SIDE + spot[3]))
    return pairs


def trade(value, axis, turn):
    return lax.ppermute(value, MESH, routes(axis, turn))


def add(*values):
    return functools.reduce(jnp.add, (v.astype(f32) for v in values)).astype(low)


def both_of(own, axis, turn):
    return jnp.stack([own, trade(own, axis, turn)])


def gather_first(own, axis):
    pair = both_of(own, axis, 0)
    return jnp.concatenate([pair, trade(pair, axis, 1)])


def gather_second(own, axis):
    pair = both_of(own, axis, 0)
    return pair, trade(pair, axis, 1)


def halves_of(kept, got):
    middle = kept.shape[0] // 2
    return add(kept[:middle], got[:middle]), add(kept[middle:], got[middle:])


tied = lax.optimization_barrier


def per_device(
    patches, mask_flags, image_tags, mask_token, group_table, qkv_weight, query_value_bias, out_weight,
    up_weight, hidden_bias, down_weight, norm_gains, norm_biases, cotangent,
):
    place = lax.axis_index("heads")
    core = lax.axis_index("section")
    first = core == 0

    rows = qkv_weight.shape[1]
    mine, other = call(
        shards_kernel, "shards",
        (core.reshape(1), qkv_weight[0].transpose(1, 0, 2), out_weight[0].T, up_weight[0], down_weight[0].T),
        [shaped((rows, LAYER), low)] * 2, {("in", 0): SMALL}, 2, grid=1, limit=60 * 2**20,
    )
    other = swap(other)
    zero, one = jnp.where(first, mine, other), jnp.where(first, other, mine)

    def by_pair(wide):
        return [wide[:, s * 2 * HALF + k * 2 * PAIR : s * 2 * HALF + (k + 1) * 2 * PAIR] for k in range(STEPS) for s in (0, 1)]

    shard = jnp.concatenate([one[:, :FEED], zero[:, :FEED], *by_pair(one[:, FEED:])], axis=1)
    weights = lax.all_gather(shard, "dp", axis=0, tiled=True)
    pieces = gather_first(zero[:, FEED : FEED + 2 * HALF], 0), gather_first(zero[:, FEED + 2 * HALF :], 1)
    pieces = (*gather_second(pieces[0], 1), *gather_second(pieces[1], 0))
    later = (patches, mask_flags, image_tags, mask_token, group_table, cotangent, norm_gains, norm_biases, query_value_bias, hidden_bias)
    later, _ = tied((later, shard))
    patches, mask_flags, image_tags, mask_token, group_table, cotangent, norm_gains, norm_biases, query_value_bias, hidden_bias = later

    x, y = lax.axis_index("dp") // SIDE, lax.axis_index("dp") % SIDE
    flips = jnp.where(first, jnp.array([0, 1, 3, 2], jnp.int32), jnp.array([0, 3, 1, 2], jnp.int32))
    slots = jnp.concatenate([x ^ flips, y ^ flips])
    order = jnp.argmax((place ^ flips)[None, :] == jnp.arange(SIDE, dtype=jnp.int32)[:, None], axis=1).astype(jnp.int32)

    def half_of(vector):
        return jnp.where(first, vector[..., : vector.shape[-1] // 2], vector[..., vector.shape[-1] // 2 :])

    vectors = lax.all_gather(
        jnp.concatenate([norm_gains[0], norm_biases[0], query_value_bias[0], hidden_bias[0].reshape(4, D)]),
        "section", axis=0,
    )
    norms, offsets, bias_ups = [], [], []
    for layer in range(2):
        v = vectors[layer]
        norms.append(jnp.pad(v[:6], ((0, 2), (0, 0))))
        query, value = half_of(v[6:8]).reshape(2, STEPS, PAIR)
        offsets.append(jnp.stack([query, jnp.zeros_like(query), value], axis=1).reshape(1, 3 * HALF))
        bias_ups.append(half_of(v[8:12].reshape(1, FF)))

    def own(rows_of):
        return lax.dynamic_slice_in_dim(rows_of, place * PATCHES, PATCHES, 0)

    def padded(value):
        return jnp.pad(value, ((0, ROWS - PATCHES), (0, 0)))

    masked = lax.dynamic_slice_in_dim(mask_flags, place, 1, 0).reshape(PATCHES, 1).astype(f32)
    tag = lax.dynamic_slice_in_dim(image_tags, place, 1, 0)
    onehot = (tag[:, None] == jnp.arange(GROUPS, dtype=jnp.int32)[None, :]).astype(f32)
    image_row = jnp.sum(onehot.T * group_table, axis=0, keepdims=True)
    stream_zero = padded(jnp.where(masked > 0, mask_token[None, :], own(patches).astype(f32)) + image_row)
    seed, masked = padded(own(cotangent)), padded(masked)

    attn_zero, normed, packed, lse, context, part = attention_zero_call(slots, stream_zero, norms[0], offsets[0], pieces)
    middle, normed_two, upper, mixed = forward_call(stream_zero, part, swap(part), norms[0], bias_ups[0], weights)
    kept = (middle, norms[0], normed, packed, lse, context, attn_zero)
    stream_one, normed, packed, lse, context, part = attention_one_call(
        middle, mixed, swap(mixed), norms[0][5:6], norms[1], offsets[1], weights
    )
    grads, middle, mixed, part, bias_one, turn_rows = turn_call(
        seed, stream_one, part, swap(part), norms[1], bias_ups[1], weights
    )
    grads, grad_middle, part, rows_one, sums_one = attention_back_one_call(
        seed, part, swap(part), middle, norms[1], normed, packed, lse, context, weights, grads
    )
    grads, part, bias_zero, back_rows, branch = backward_call(
        (grad_middle, part, swap(part), stream_one, norms[1]), normed_two, upper, weights, grads
    )
    joined = lax.psum_scatter(grads, "dp", scatter_dimension=0, tiled=True)
    (zero, sent, zero_too, sent_too), (grad_middle, part, rows_zero, sums_zero) = attention_back_zero_call(
        slots, branch, part, swap(part), *kept
    )
    rows_out, vectors, _ = call(
        last_kernel, "last",
        (
            core.reshape(1), grad_middle, part, swap(part), stream_zero, norms[0], masked, tag, middle, mixed, swap(mixed),
            norms[1][5:6], rows_one, sums_one, turn_rows, bias_one, rows_zero, sums_zero, back_rows, bias_zero,
        ),
        [STREAM_LOW, shaped((BLOCK, D), low), shaped((32, D))], {("in", 0): SMALL, ("in", 7): SMALL}, 3, grid=1,
    )

    def trade_with(sent, vectors, axis, turn):
        got = trade(jnp.concatenate([sent.reshape(-1, BLOCK, D), vectors[None]]), axis, turn)
        return got[:-1].reshape(sent.shape), add(vectors, got[-1])

    (got, vectors), got_too = trade_with(sent, vectors, 0, 1), trade(sent_too, 1, 1)
    got, got_too, rows_out = tied((got, got_too, rows_out))
    ends = both_of(rows_out, 2, 0)
    (zero, sent), (zero_too, sent_too) = halves_of(zero, got), halves_of(zero_too, got_too)
    (got, vectors), got_too = trade_with(sent, vectors, 0, 0), trade(sent_too, 1, 0)
    got, got_too, ends = tied((got, got_too, ends))
    ends = jnp.concatenate([ends, trade(ends, 2, 1)])
    (zero, sent), (zero_too, sent_too) = halves_of(zero[0], got[0]), halves_of(zero_too[0], got_too[0])
    (got, vectors), got_too = trade_with(sent, vectors, 1, 1), trade(sent_too, 0, 1)
    (zero, sent), (zero_too, sent_too) = halves_of(zero, got), halves_of(zero_too, got_too)
    (got, vectors), got_too = trade_with(sent, vectors, 1, 0), trade(sent_too, 0, 0)
    attn_sum = jnp.concatenate([*by_pair(jnp.concatenate([add(zero[0], got[0]), add(zero_too[0], got_too[0])], axis=1)), vectors], axis=1)

    def z_sum(value):
        value = add(value, trade(value, 2, 0))
        return add(value, trade(value, 2, 1))

    attn_sum = z_sum(attn_sum)
    (ends_here,) = call(
        ends_kernel, "ends", (order, ends), [shaped((SIDE * PATCHES, D))], {("in", 0): SMALL}, 2, grid=1
    )
    joined, attn_sum, ends_here = tied((joined, attn_sum, ends_here))

    joined = z_sum(joined)
    zero = jnp.concatenate([joined[:, FEED : 2 * FEED], attn_sum], axis=1)
    one = jnp.concatenate([joined[:, :FEED], joined[:, 2 * FEED :], attn_sum[:, ATTN:]], axis=1)
    mine = jnp.where(first, zero, one)
    other = swap(jnp.where(first, one, zero))
    grad_qkv, grad_out, grad_up, grad_down, grad_qv, grad_hidden, grad_gains, grad_biases, grad_token, grad_table = call(
        grads_kernel, "grads", (core.reshape(1), jnp.where(first, mine, other), jnp.where(first, other, mine)),
        [
            shaped((3, rows, D)), shaped((rows, D)), shaped((rows, FF)), shaped((rows, FF)), shaped((2, D)), shaped((1, FF)),
            shaped((2, D)), shaped((4, D)), shaped((1, HALF)), shaped((GROUPS, HALF)),
        ],
        {("in", 0): SMALL}, 2, grid=1,
    )
    return (
        ends_here[None], grad_qkv.transpose(1, 0, 2)[None], grad_qv[None], grad_out.T[None], grad_up[None], grad_hidden,
        grad_down.T[None], grad_gains[None], grad_biases[None], grad_token[0], grad_table,
    )


def solution(mesh):
    in_specs = (
        P("dp", None), P("dp", None), P("dp"), P(), P(),
        P("section", "dp", None, None), P("section", None, None), P("section", None, "dp"),
        P("section", "dp", None), P("section", None), P("section", None, "dp"),
        P("section", None, None), P("section", None, None), P("dp", None),
    )
    out_specs = (
        P("section", "dp", None), P("section", "dp", None, None), P("section", None, None),
        P("section", None, "dp"), P("section", "dp", None), P("section", None), P("section", None, "dp"),
        P("section", None, None), P("section", None, None), P("section"), P(None, "section"),
    )
    return jax.shard_map(per_device, mesh=mesh, in_specs=in_specs, out_specs=out_specs, check_vma=False)
```

```python
import functools

import jax
import jax.numpy as jnp
from jax import lax
from jax.experimental import pallas as pl
from jax.experimental.pallas import tpu as pltpu
from jax.sharding import PartitionSpec as P

D = 768
HD = 64
FF = 3072
PATCHES = 196
ROWS = 208
GROUPS = 8
HALF = D // 2
HALF_FF = FF // 2
PAIR = 2 * HD
STEPS = 3
CHUNK = HALF_FF // STEPS
FEED = 2 * HALF_FF
ATTN = 4 * HALF
LAYER = FEED + ATTN
GATHERED = LAYER + ATTN
JOINED = LAYER + FEED
QUARTER = HALF_FF // 4
SIDE = 4
BLOCK = D // SIDE**2
MESH = ("section", "dp", "heads")
SWAP = [(0, 1), (1, 0)]
LIMIT = 48 * 2**20
ALL = 60 * 2**20
SCALE = HD ** (-0.5)
epsilon = 1e-06
f32 = jnp.float32
low = jnp.bfloat16


def dot(left, right):
    return jnp.dot(left, right, preferred_element_type=f32)


def dot_t(left, right):
    return lax.dot_general(left, right, (((1,), (1,)), ((), ())), preferred_element_type=f32)


def t_dot(left, right):
    return lax.dot_general(left, right, (((0,), (0,)), ((), ())), preferred_element_type=f32)


def both(own, other):
    return own[...].astype(f32) + other[...].astype(f32)


def column_sum(value):
    return jnp.sum(value.astype(f32), axis=0, keepdims=True)


def stats(value):
    average = jnp.mean(value, axis=-1, keepdims=True)
    centred = value - average
    rate = lax.rsqrt(jnp.mean(centred * centred, axis=-1, keepdims=True) + epsilon)
    return centred * rate, rate


def norm_back(value, gain, grad):
    x, rate = stats(value)
    scaled = grad * gain
    inner = scaled - jnp.mean(scaled, axis=-1, keepdims=True)
    inner = inner - x * jnp.mean(scaled * x, axis=-1, keepdims=True)
    return rate * inner, column_sum(grad * x), column_sum(grad)


def gauss(value):
    return 0.5 + 0.5 * lax.erf(value * 0.7071067811865476), jnp.exp(value * value * -0.5) * 0.3989422804014327


def head_masks():
    left = lax.broadcasted_iota(jnp.int32, (ROWS, PAIR), 1) < HD
    nothing = jnp.zeros((ROWS, PAIR), low)
    return left, (lambda rows: jnp.where(left, rows, nothing), lambda rows: jnp.where(left, nothing, rows))


def raw_scores(key_rows, queries):
    scores = dot_t(key_rows, queries) * SCALE
    return jnp.where(lax.broadcasted_iota(jnp.int32, scores.shape, 0) < PATCHES, scores, -1e30)


def block_copies(slots, blocks, joined, sem, start, size, outwards=False):
    copies = []
    for i in range(SIDE):
        for j in range(SIDE):
            row = pl.multiple_of(slots[i] * (SIDE * BLOCK) + slots[SIDE + j] * BLOCK, 16)
            for half in range(2):
                outer, inner = (i, j) if outwards == (half == 0) else (j, i)
                ends = (
                    blocks[2 * half + outer // 2].at[outer % 2, inner, :, pl.ds(start, size)],
                    joined.at[pl.ds(row, BLOCK), pl.ds(half * size, size)],
                )
                copies.append(pltpu.make_async_copy(*(reversed(ends) if outwards else ends), sem))
    return copies


def all_landed(joined, sem):
    pltpu.make_async_copy(joined, joined, sem).wait()


def start_all(copies):
    for copy in copies:
        copy.start()


def wait_all(copies):
    for copy in copies:
        copy.wait()


def column_copies(whole, parts, sems, start, size, outwards=False):
    copies = []
    for k in range(parts.shape[0]):
        at = start[k] if isinstance(start, list) else start + k * size
        ends = whole.at[:, pl.ds(at, size)], parts.at[k]
        copies.append(pltpu.make_async_copy(*(reversed(ends) if outwards else ends), sems.at[k]))
    return copies


def pair_forward(packed, write_lse):
    left, choose = head_masks()
    queries, keys, values = (packed[:, k * PAIR : (k + 1) * PAIR] for k in range(3))
    found = []
    for head in range(2):
        scores = raw_scores(keys, choose[head](queries))
        summit = jnp.max(scores, axis=0, keepdims=True)
        raised = jnp.exp(scores - summit)
        whole = jnp.sum(raised, axis=0, keepdims=True)
        write_lse(head, summit + jnp.log(whole))
        found.append(t_dot((raised * (1.0 / whole)).astype(low), values))
    return jnp.where(left, found[0], found[1]).astype(low)


def pair_backward(packed, lse, grad_pair, grad_packed):
    left, choose = head_masks()
    queries, keys, values = (packed[:, k * PAIR : (k + 1) * PAIR] for k in range(3))
    found = []
    for head in range(2):
        soft = jnp.exp(raw_scores(keys, choose[head](queries)) - lse[head : head + 1, :])
        grad_probs = dot_t(values, choose[head](grad_pair))
        within = jnp.sum(grad_probs * soft, axis=0, keepdims=True)
        grad_scores = (soft * (grad_probs - within)).astype(low)
        found.append((t_dot(grad_scores, keys) * SCALE, dot(grad_scores, queries) * SCALE, dot(soft.astype(low), grad_pair)))
    for k in range(3):
        grad_packed[:, k * PAIR : (k + 1) * PAIR] = jnp.where(left, found[0][k], found[1][k]).astype(low)
    return grad_packed[...]


def attention_kernel(second, *refs):
    if second:
        base, own, other, last_bias, norms, offset, weights, stream_out, *refs = refs
    else:
        base, norms, offset, weights, *refs = refs
    normed_out, packed_out, lse_out, context_out, part_out, weight, sems = refs
    copies = column_copies(weights, weight, sems, FEED + (ATTN if second else 0), 4 * PAIR)
    start_all(copies)
    stream = base[...]
    if second:
        stream = (stream + (both(own, other) + last_bias[...])).astype(low).astype(f32)
        stream_out[...] = stream
    normed = (stats(stream)[0] * norms[0:1] + norms[2:3]).astype(low)
    normed_out[...] = normed
    total = 0.0
    for k in range(STEPS):
        copies[k].wait()
        at = slice(k * 3 * PAIR, (k + 1) * 3 * PAIR)
        packed = (dot(normed, weight[k, :, : 3 * PAIR]) + offset[:, at]).astype(low)
        packed_out[:, at] = packed

        def write_lse(head, row):
            lse_out[k, head : head + 1, :] = row

        context = pair_forward(packed, write_lse)
        context_out[:, k * PAIR : (k + 1) * PAIR] = context
        total = total + dot_t(context, weight[k, :, 3 * PAIR :])
    part_out[...] = total.astype(low)


def forward_kernel(
    stream, own, other, norms, bias, weights, middle_out, normed_out, upper_out, part_out, weight, kept, sems, out_sems
):
    copies = column_copies(weights, weight, sems, 0, 2 * CHUNK)
    start_all(copies)
    leaving = column_copies(upper_out, kept, out_sems, 0, CHUNK, True)
    middle = stream[...] + (both(own, other) + norms[3:4])
    middle_out[...] = middle
    normed = (stats(middle)[0] * norms[1:2] + norms[4:5]).astype(low)
    normed_out[...] = normed
    total = 0.0
    for k in range(STEPS):
        copies[k].wait()
        upper = dot(normed, weight[k, :, :CHUNK]) + bias[:, k * CHUNK : (k + 1) * CHUNK]
        kept[k] = upper
        leaving[k].start()
        hidden = (upper * gauss(upper)[0]).astype(low)
        total = total + dot_t(hidden, weight[k, :, CHUNK:])
    part_out[...] = total.astype(low)
    for copy in leaving:
        copy.wait()


def turn_kernel(
    slots, branch, stream, own, other, norms, bias, near, far,
    grads_out, middle_out, mixed_out, part_out, bias_out, rows_out, weight, grads, sems, out_sems,
):
    for k in range(SIDE):
        pieces = [(near, far)[k // 2].at[k % 2, p] for p in range(SIDE)]
        start_all(block_copies(slots, pieces, weight.at[k], sems.at[k], 0, QUARTER))
    units = [pl.multiple_of(slots[2 * SIDE + k] * QUARTER, 128) for k in range(SIDE)]
    leaving = column_copies(grads_out, grads, out_sems, [pl.multiple_of(2 * u, 256) for u in units], 2 * QUARTER, True)
    middle = stream[...] + (both(own, other) + norms[3:4])
    middle_out[...] = middle
    normed = (stats(middle)[0] * norms[1:2] + norms[4:5]).astype(low)
    rows = branch[...]
    rows_out[2:3] = column_sum(rows)
    total = mixed = 0.0
    for k in range(SIDE):
        at = pl.ds(units[k], QUARTER)
        all_landed(weight.at[k], sems.at[k])
        upper = dot(normed, weight[k, :, :QUARTER]) + bias[:, at]
        share, density = gauss(upper)
        hidden = (upper * share).astype(low)
        grad_upper = (dot(rows, weight[k, :, QUARTER:]) * (share + upper * density)).astype(low)
        total = total + dot_t(grad_upper, weight[k, :, :QUARTER])
        grads[k, :, :QUARTER] = t_dot(normed, grad_upper).astype(low)
        grads[k, :, QUARTER:] = t_dot(rows, hidden).astype(low)
        leaving[k].start()
        bias_out[:, at] = column_sum(grad_upper)
        mixed = mixed + dot_t(hidden, weight[k, :, QUARTER:])
    part_out[...] = total.astype(low)
    mixed_out[...] = mixed.astype(low)
    wait_all(leaving)


def backward_kernel(
    grad, own, other, stream, gains, normed_in, uppers, weights, _,
    grads_out, part_out, bias_out, rows_out, branch, weight, upper, grads, sems, upper_sems, out_sems,
):
    copies = column_copies(weights, weight, sems, 0, 2 * CHUNK)
    entering = column_copies(uppers, upper, upper_sems, 0, CHUNK)
    for pair in zip(copies, entering):
        for copy in pair:
            copy.start()
    leaving = column_copies(grads_out, grads, out_sems, FEED, 2 * CHUNK, True)
    into, gain, shift = norm_back(stream[...], gains[0:1], both(own, other))
    rows = (grad[...] + into).astype(low)
    branch[...] = rows
    rows_out[0:1] = gain
    rows_out[1:2] = shift
    rows_out[2:3] = column_sum(rows)
    normed = normed_in[...]
    total = 0.0
    for k in range(STEPS):
        entering[k].wait()
        copies[k].wait()
        upper_now = upper[k]
        share, density = gauss(upper_now)
        hidden = (upper_now * share).astype(low)
        grad_upper = (dot(rows, weight[k, :, CHUNK:]) * (share + upper_now * density)).astype(low)
        total = total + dot_t(grad_upper, weight[k, :, :CHUNK])
        grads[k, :, :CHUNK] = t_dot(normed, grad_upper).astype(low)
        grads[k, :, CHUNK:] = t_dot(rows, hidden).astype(low)
        leaving[k].start()
        bias_out[:, k * CHUNK : (k + 1) * CHUNK] = column_sum(grad_upper)
    part_out[...] = total.astype(low)
    for copy in leaving:
        copy.wait()


def attention_back_kernel(second, *refs):
    if not second:
        slots, *refs = refs
    branch, own, other, middle, norms, normed_in, packed, lse, context, weights, *refs = refs
    if second:
        _, grads_out, *refs = refs
    else:
        blocks, refs = refs[:SIDE], refs[SIDE:]
    middle_out, part_out, rows_out, packed_out, weight, grads, grad_packed, sems, out_sems = refs
    copies = column_copies(weights, weight, sems, FEED + (ATTN if second else 0), 4 * PAIR)
    start_all(copies)
    if second:
        leaving = column_copies(grads_out, grads, out_sems, 2 * FEED, 4 * PAIR, True)
    into, gain, shift = norm_back(middle[...], norms[1:2], both(own, other))
    grad_middle = branch[...].astype(f32) + into
    middle_out[...] = grad_middle
    attn = grad_middle.astype(low)
    rows_out[0:1] = gain
    rows_out[1:2] = shift
    rows_out[2:3] = column_sum(attn)
    normed = normed_in[...]
    total = 0.0
    for k in range(STEPS):
        at = slice(k * 3 * PAIR, (k + 1) * 3 * PAIR)
        copies[k].wait()
        grad_pair = dot(attn, weight[k, :, 3 * PAIR :]).astype(low)
        rows = pair_backward(packed[:, at], lse[k], grad_pair, grad_packed)
        total = total + dot_t(rows, weight[k, :, : 3 * PAIR])
        grads[k, :, : 3 * PAIR] = t_dot(normed, rows).astype(low)
        grads[k, :, 3 * PAIR :] = t_dot(attn, context[:, k * PAIR : (k + 1) * PAIR]).astype(low)
        if second:
            leaving[k].start()
        else:
            start_all(block_copies(slots, blocks, grads.at[k], out_sems.at[k], 2 * k * PAIR, 2 * PAIR, True))
        packed_out[:, at] = column_sum(rows)
    part_out[...] = total.astype(low)
    for k in range(STEPS):
        if second:
            leaving[k].wait()
        else:
            all_landed(grads.at[k], out_sems.at[k])


def last_kernel(
    core, grad_middle, own, other, stream, norms, masked, tag, middle, mixed, mixed_other, last_bias,
    rows_one, sums_one, turn_rows, bias_one, rows_zero, sums_zero, back_rows, bias_zero, rows_out, vectors_low_out, vectors_out,
):
    into, gain, shift = norm_back(stream[...], norms[0:1], both(own, other))
    grad_zero = grad_middle[...] + into
    hidden = masked[...] > 0.5
    final = middle[...] + (both(mixed, mixed_other) + last_bias[...])
    first = core[0] == 0
    rows_out[...] = jnp.where(first, jnp.where(hidden, 0.0, grad_zero), final).astype(low)
    for at, gain_one, shift_one, attn_rows, feed_rows, sums, bias in (
        (0, gain, shift, rows_zero, back_rows, sums_zero, bias_zero),
        (9, back_rows[0:1], back_rows[1:2], rows_one, turn_rows, sums_one, bias_one),
    ):
        for k, row in enumerate((gain_one, attn_rows[0:1], shift_one, attn_rows[2:3], attn_rows[1:2], feed_rows[2:3])):
            vectors_out[at + k : at + k + 1] = row
        for k in range(STEPS):
            for part in range(2):
                to = part * HALF + k * PAIR
                vectors_out[at + 6 : at + 7, to : to + PAIR] = sums[:, (3 * k + 2 * part) * PAIR : (3 * k + 2 * part + 1) * PAIR]
        for k in range(2):
            vectors_out[at + 7 + k : at + 8 + k] = bias[:, k * D : (k + 1) * D]
    vectors_out[18:19] = column_sum(jnp.where(hidden, grad_zero, 0.0))
    table = column_sum(grad_zero)
    for group in range(GROUPS):
        vectors_out[19 + group : 20 + group] = jnp.where(tag[0] == group, table, 0.0)
    vectors_out[27:32] = jnp.zeros((5, D), f32)
    vectors_low_out[...] = jnp.zeros((BLOCK, 2 * HALF), low)
    vectors_low_out[0:32, 0:D] = vectors_out[...].astype(low)


def ends_kernel(order, parts, out):
    for k in range(SIDE):
        out[k * PATCHES : (k + 1) * PATCHES] = parts[order[k]].astype(f32)[:PATCHES]


def feed_columns(layer):
    size = QUARTER if layer == 1 else CHUNK
    return [(2 * at, slice(at, at + size), size) for at in range(0, HALF_FF, size)]


def attn_columns():
    return [[FEED + (4 * k + c) * PAIR for c in range(4)] for k in range(STEPS)]


def shards_kernel(core, qkv, out, up, down, mine_out, sent_out):
    def fill(layer, half, target):
        for to, units, size in feed_columns(layer):
            units = slice(units.start + half * HALF_FF, units.stop + half * HALF_FF)
            target[:, to : to + size] = up[:, units].astype(low)
            target[:, to + size : to + 2 * size] = down[:, units].astype(low)
        for k, spots in enumerate(attn_columns()):
            at = slice(half * HALF + k * PAIR, half * HALF + (k + 1) * PAIR)
            for to, rows in zip(spots, (qkv[0, :, at], qkv[1, :, at], qkv[2, :, at], out[:, at])):
                target[:, to : to + PAIR] = rows.astype(low)

    for index in range(2):
        @pl.when(core[0] == index)
        def _():
            fill(index, index, mine_out)
            fill(index, 1 - index, sent_out)


def grads_kernel(
    core, first_half, second_half,
    qkv_out, out_out, up_out, down_out, qv_out, hidden_out, gains_out, biases_out, token_out, table_out,
):
    halves = first_half, second_half
    shared = first_half[:, LAYER : LAYER + D].astype(f32)

    def fill(layer, half, part):
        for at, units, size in feed_columns(layer):
            units = slice(units.start + half * HALF_FF, units.stop + half * HALF_FF)
            up_out[:, units] = part[:, at : at + size].astype(f32)
            down_out[:, units] = part[:, at + size : at + 2 * size].astype(f32)
        for k, spots in enumerate(attn_columns()):
            to = slice(half * HALF + k * PAIR, half * HALF + (k + 1) * PAIR)
            for c in range(3):
                qkv_out[c, :, to] = part[:, spots[c] : spots[c] + PAIR].astype(f32)
            out_out[:, to] = part[:, spots[3] : spots[3] + PAIR].astype(f32)

    for index in range(2):
        @pl.when(core[0] == index)
        def _():
            at = 9 * index
            gains_out[...] = shared[at : at + 2]
            biases_out[...] = shared[at + 2 : at + 6]
            token_out[...] = shared[18:19, index * HALF : (index + 1) * HALF]
            table_out[...] = shared[19 : 19 + GROUPS, index * HALF : (index + 1) * HALF]
            for h, half in enumerate(halves):
                fill(index, h, half)
                rows = half[:, LAYER : LAYER + D].astype(f32)
                for k in range(2):
                    qv_out[k : k + 1, h * HALF : (h + 1) * HALF] = rows[at + 6 : at + 7, k * HALF : (k + 1) * HALF]
                    hidden_out[:, h * HALF_FF + k * D : h * HALF_FF + (k + 1) * D] = rows[at + 7 + k : at + 8 + k]


def whole(array):
    return pl.BlockSpec(array.shape, lambda *_: (0,) * len(array.shape))


def shaped(shape, kind=f32):
    return jax.ShapeDtypeStruct(shape, kind)


def call(kernel, name, operands, outs, specs, micros, alias=None, scratch=(), limit=LIMIT):
    def spec(key, array):
        return specs.get(key) or whole(array)

    return pl.pallas_call(
        kernel,
        name=name,
        grid=(1,),
        in_specs=[spec(("in", k), a) for k, a in enumerate(operands)],
        out_specs=[spec(("out", k), a) for k, a in enumerate(outs)],
        out_shape=outs,
        scratch_shapes=scratch,
        input_output_aliases=alias or {},
        cost_estimate=pl.CostEstimate(flops=0, bytes_accessed=int(micros * 3.6e6), transcendentals=0),
        compiler_params=pltpu.CompilerParams(vmem_limit_bytes=limit),
    )(*operands)


SMALL = pl.BlockSpec(memory_space=pltpu.SMEM)
LEFT = pl.BlockSpec(memory_space=pl.ANY)


STREAM = shaped((ROWS, D))
STREAM_LOW = shaped((ROWS, D), low)


DMA = pltpu.SemaphoreType.DMA((STEPS,))
FEED_PARTS = pltpu.VMEM((STEPS, D, 2 * CHUNK), low)
ATTN_PARTS = pltpu.VMEM((STEPS, D, 4 * PAIR), low)
UPPER_PARTS = pltpu.VMEM((STEPS, ROWS, CHUNK), f32)
ATTN_KEPT = [STREAM_LOW, shaped((ROWS, 3 * HALF), low), shaped((STEPS, 8, ROWS)), shaped((ROWS, HALF), low), STREAM_LOW]
JOINED_GRADS = shaped((D, JOINED), low)


def attention_call(layer, entry, norms, offset, weights):
    second = layer == 1
    operands = (*entry, norms, offset, weights)
    return call(
        functools.partial(attention_kernel, second), f"attention_{layer}", operands, [STREAM, *ATTN_KEPT] if second else ATTN_KEPT,
        {("in", len(operands) - 1): LEFT}, 4, scratch=[ATTN_PARTS, DMA],
    )


def forward_call(stream, part, part_other, norms, bias_up, weights):
    return call(
        forward_kernel, "feed_0", (stream, part, part_other, norms, bias_up, weights),
        [STREAM, STREAM_LOW, shaped((ROWS, HALF_FF)), STREAM_LOW], {("in", 5): LEFT, ("out", 2): LEFT}, 4,
        scratch=[FEED_PARTS, UPPER_PARTS, DMA, DMA],
    )


def turn_call(slots, branch, stream, part, part_other, norms, bias_up, near, far):
    parts, sems = pltpu.VMEM((SIDE, D, 2 * QUARTER), low), pltpu.SemaphoreType.DMA((SIDE,))
    return call(
        turn_kernel, "feed_1", (slots, branch, stream, part, part_other, norms, bias_up, near, far),
        [JOINED_GRADS, STREAM, STREAM_LOW, STREAM_LOW, shaped((1, HALF_FF)), shaped((8, D))],
        {("in", 0): SMALL, ("in", 7): LEFT, ("in", 8): LEFT, ("out", 0): LEFT}, 9, scratch=[parts, parts, sems, sems],
    )


def backward_call(entry, normed, upper, weights, grads):
    return call(
        backward_kernel, "feed_back_0", (*entry, normed, upper, weights, grads),
        [JOINED_GRADS, STREAM_LOW, shaped((1, HALF_FF)), shaped((8, D)), STREAM_LOW],
        {("in", 6): LEFT, ("in", 7): LEFT, ("in", 8): LEFT, ("out", 0): LEFT}, 6, alias={8: 0},
        scratch=[FEED_PARTS, UPPER_PARTS, FEED_PARTS, DMA, DMA, DMA],
    )


def attention_back_call(layer, entry, branch, part, part_other, middle, norms, normed, packed, lse, context, weights, grads):
    second = layer == 1
    operands = (*entry, branch, part, part_other, middle, norms, normed, packed, lse, context, weights, *grads)
    outs = [JOINED_GRADS] if second else [shaped((2, SIDE, BLOCK, 2 * HALF), low)] * SIDE
    count, last = len(outs), len(operands) - 1
    specs = {("in", k): LEFT for k in ((last - 1, last) if second else (last,))}
    if not second:
        specs["in", 0] = SMALL
    specs.update({("out", k): LEFT for k in range(count)})
    made = call(
        functools.partial(attention_back_kernel, second), f"attention_back_{layer}", operands,
        [*outs, STREAM, STREAM_LOW, shaped((8, D)), shaped((1, 3 * HALF))], specs, 7, alias={last: 0} if second else None,
        scratch=[ATTN_PARTS, ATTN_PARTS, pltpu.VMEM((ROWS, 3 * PAIR), low), DMA, DMA],
    )
    return made[:count], made[count:]


def swap(value):
    return lax.ppermute(value, "section", SWAP)


def routes(axis, turn):
    pairs = []
    for place in range(2 * SIDE**3):
        spot = [place // SIDE**3, place // SIDE**2 % SIDE, place // SIDE % SIDE, place % SIDE]
        spot[axis + 1] ^= 1 if spot[0] == turn else 3
        pairs.append((place, ((spot[0] * SIDE + spot[1]) * SIDE + spot[2]) * SIDE + spot[3]))
    return pairs


def trade(value, axis, turn):
    return lax.ppermute(value, MESH, routes(axis, turn))


def add(*values):
    return functools.reduce(jnp.add, (v.astype(f32) for v in values)).astype(low)


def both_of(own, axis, turn):
    return jnp.stack([own, trade(own, axis, turn)])


def gather_first(own, axis):
    pair = both_of(own, axis, 0)
    return jnp.concatenate([pair, trade(pair, axis, 1)])


def gather_second(own, axis):
    pair = both_of(own, axis, 0)
    return pair, trade(pair, axis, 1)


def halves_of(kept, got):
    middle = kept.shape[0] // 2
    return add(kept[:middle], got[:middle]), add(kept[middle:], got[middle:])


tied = lax.optimization_barrier


def per_device(
    patches, mask_flags, image_tags, mask_token, group_table, qkv_weight, query_value_bias, out_weight,
    up_weight, hidden_bias, down_weight, norm_gains, norm_biases, cotangent,
):
    place = lax.axis_index("heads")
    core = lax.axis_index("section")
    first = core == 0

    x, y = lax.axis_index("dp") // SIDE, lax.axis_index("dp") % SIDE
    flips = jnp.where(first, jnp.array([0, 1, 3, 2], jnp.int32), jnp.array([0, 3, 1, 2], jnp.int32))
    slots = jnp.concatenate([x ^ flips, y ^ flips, place ^ flips])
    order = jnp.argmax((place ^ flips)[None, :] == jnp.arange(SIDE, dtype=jnp.int32)[:, None], axis=1).astype(jnp.int32)

    rows = qkv_weight.shape[1]
    mine, other = call(
        shards_kernel, "shards",
        (core.reshape(1), qkv_weight[0].transpose(1, 0, 2), out_weight[0].T, up_weight[0], down_weight[0].T),
        [shaped((rows, LAYER), low)] * 2, {("in", 0): SMALL}, 2, limit=ALL,
    )
    other = swap(other)
    zero, one = jnp.where(first, mine, other), jnp.where(first, other, mine)

    shard = jnp.concatenate([zero, one[:, FEED:]], axis=1)
    weights = lax.all_gather(shard, "dp", axis=0, tiled=True)
    quarter = lax.dynamic_slice_in_dim(one, place * 2 * QUARTER, 2 * QUARTER, 1)
    near = gather_first(quarter[:, :QUARTER], 0), gather_first(quarter[:, QUARTER:], 1)
    near = jnp.stack([*gather_second(near[0], 1), *gather_second(near[1], 0)])
    near = both_of(near, 2, 0)
    far = trade(near, 2, 1)
    later = (patches, mask_flags, image_tags, mask_token, group_table, cotangent, norm_gains, norm_biases, query_value_bias, hidden_bias)
    later, _ = tied((later, near))
    patches, mask_flags, image_tags, mask_token, group_table, cotangent, norm_gains, norm_biases, query_value_bias, hidden_bias = later

    def half_of(vector):
        return jnp.where(first, vector[..., : vector.shape[-1] // 2], vector[..., vector.shape[-1] // 2 :])

    vectors = lax.all_gather(
        jnp.concatenate([norm_gains[0], norm_biases[0], query_value_bias[0], hidden_bias[0].reshape(4, D)]),
        "section", axis=0,
    )
    norms, offsets, bias_ups = [], [], []
    for layer in range(2):
        v = vectors[layer]
        norms.append(jnp.pad(v[:6], ((0, 2), (0, 0))))
        query, value = half_of(v[6:8]).reshape(2, STEPS, PAIR)
        offsets.append(jnp.stack([query, jnp.zeros_like(query), value], axis=1).reshape(1, 3 * HALF))
        bias_ups.append(half_of(v[8:12].reshape(1, FF)))

    def own(rows_of):
        return lax.dynamic_slice_in_dim(rows_of, place * PATCHES, PATCHES, 0)

    def padded(value):
        return jnp.pad(value, ((0, ROWS - PATCHES), (0, 0)))

    masked = lax.dynamic_slice_in_dim(mask_flags, place, 1, 0).reshape(PATCHES, 1).astype(f32)
    tag = lax.dynamic_slice_in_dim(image_tags, place, 1, 0)
    onehot = (tag[:, None] == jnp.arange(GROUPS, dtype=jnp.int32)[None, :]).astype(f32)
    image_row = jnp.sum(onehot.T * group_table, axis=0, keepdims=True)
    stream_zero = padded(jnp.where(masked > 0, mask_token[None, :], own(patches).astype(f32)) + image_row)
    seed, masked = padded(own(cotangent)), padded(masked)

    normed, packed, lse, context, part = attention_call(0, (stream_zero,), norms[0], offsets[0], weights)
    middle, normed_two, upper, mixed = forward_call(stream_zero, part, swap(part), norms[0], bias_ups[0], weights)
    kept = (middle, norms[0], normed, packed, lse, context)
    stream_one, normed, packed, lse, context, part = attention_call(
        1, (middle, mixed, swap(mixed), norms[0][5:6]), norms[1], offsets[1], weights
    )
    grads, middle, mixed, part, bias_one, turn_rows = turn_call(
        slots, seed, stream_one, part, swap(part), norms[1], bias_ups[1], near, far
    )
    (grads,), (grad_middle, part, rows_one, sums_one) = attention_back_call(
        1, (), seed, part, swap(part), middle, norms[1], normed, packed, lse, context, weights, [grads]
    )
    grads, part, bias_zero, back_rows, branch = backward_call(
        (grad_middle, part, swap(part), stream_one, norms[1]), normed_two, upper, weights, grads
    )
    joined = lax.psum_scatter(grads, "dp", scatter_dimension=0, tiled=True)
    (zero, sent, zero_too, sent_too), (grad_middle, part, rows_zero, sums_zero) = attention_back_call(
        0, (slots,), branch, part, swap(part), *kept, weights, []
    )
    rows_out, vectors, _ = call(
        last_kernel, "last",
        (
            core.reshape(1), grad_middle, part, swap(part), stream_zero, norms[0], masked, tag, middle, mixed, swap(mixed),
            norms[1][5:6], rows_one, sums_one, turn_rows, bias_one, rows_zero, sums_zero, back_rows, bias_zero,
        ),
        [STREAM_LOW, shaped((BLOCK, D), low), shaped((32, D))], {("in", 0): SMALL, ("in", 7): SMALL}, 3, limit=ALL,
    )

    def trade_with(sent, vectors, axis, turn):
        got = trade(jnp.concatenate([sent.reshape(-1, BLOCK, D), vectors[None]]), axis, turn)
        return got[:-1].reshape(sent.shape), add(vectors, got[-1])

    (got, vectors), got_too = trade_with(sent, vectors, 0, 1), trade(sent_too, 1, 1)
    got, got_too, rows_out = tied((got, got_too, rows_out))
    ends = both_of(rows_out, 2, 0)
    (zero, sent), (zero_too, sent_too) = halves_of(zero, got), halves_of(zero_too, got_too)
    (got, vectors), got_too = trade_with(sent, vectors, 0, 0), trade(sent_too, 1, 0)
    got, got_too, ends = tied((got, got_too, ends))
    ends = jnp.concatenate([ends, trade(ends, 2, 1)])
    (zero, sent), (zero_too, sent_too) = halves_of(zero[0], got[0]), halves_of(zero_too[0], got_too[0])
    (got, vectors), got_too = trade_with(sent, vectors, 1, 1), trade(sent_too, 0, 1)
    (zero, sent), (zero_too, sent_too) = halves_of(zero, got), halves_of(zero_too, got_too)
    (got, vectors), got_too = trade_with(sent, vectors, 1, 0), trade(sent_too, 0, 0)
    def by_pair(wide):
        return [wide[:, s * 2 * HALF + k * 2 * PAIR : s * 2 * HALF + (k + 1) * 2 * PAIR] for k in range(STEPS) for s in (0, 1)]

    attn_sum = jnp.concatenate([*by_pair(jnp.concatenate([add(zero[0], got[0]), add(zero_too[0], got_too[0])], axis=1)), vectors], axis=1)

    def z_sum(value):
        value = add(value, trade(value, 2, 0))
        return add(value, trade(value, 2, 1))

    attn_sum = z_sum(attn_sum)
    (ends_here,) = call(
        ends_kernel, "ends", (order, ends), [shaped((SIDE * PATCHES, D))], {("in", 0): SMALL}, 2
    )
    joined, attn_sum, ends_here = tied((joined, attn_sum, ends_here))

    joined = z_sum(joined)
    zero = jnp.concatenate([joined[:, FEED : 2 * FEED], attn_sum], axis=1)
    one = jnp.concatenate([joined[:, :FEED], joined[:, 2 * FEED :], attn_sum[:, ATTN:]], axis=1)
    mine = jnp.where(first, zero, one)
    other = swap(jnp.where(first, one, zero))
    grad_qkv, grad_out, grad_up, grad_down, grad_qv, grad_hidden, grad_gains, grad_biases, grad_token, grad_table = call(
        grads_kernel, "grads", (core.reshape(1), jnp.where(first, mine, other), jnp.where(first, other, mine)),
        [
            shaped((3, rows, D)), shaped((rows, D)), shaped((rows, FF)), shaped((rows, FF)), shaped((2, D)), shaped((1, FF)),
            shaped((2, D)), shaped((4, D)), shaped((1, HALF)), shaped((GROUPS, HALF)),
        ],
        {("in", 0): SMALL}, 2,
    )
    return (
        ends_here[None], grad_qkv.transpose(1, 0, 2)[None], grad_qv[None], grad_out.T[None], grad_up[None], grad_hidden,
        grad_down.T[None], grad_gains[None], grad_biases[None], grad_token[0], grad_table,
    )


def solution(mesh):
    in_specs = (
        P("dp", None), P("dp", None), P("dp"), P(), P(),
        P("section", "dp", None, None), P("section", None, None), P("section", None, "dp"),
        P("section", "dp", None), P("section", None), P("section", None, "dp"),
        P("section", None, None), P("section", None, None), P("dp", None),
    )
    out_specs = (
        P("section", "dp", None), P("section", "dp", None, None), P("section", None, None),
        P("section", None, "dp"), P("section", "dp", None), P("section", None), P("section", None, "dp"),
        P("section", None, None), P("section", None, None), P("section"), P(None, "section"),
    )
    return jax.shard_map(per_device, mesh=mesh, in_specs=in_specs, out_specs=out_specs, check_vma=False)
```

```python
import functools

import jax
import jax.numpy as jnp
from jax import lax
from jax.experimental import pallas as pl
from jax.experimental.pallas import tpu as pltpu
from jax.sharding import PartitionSpec as P

D = 768
HD = 64
FF = 3072
PATCHES = 196
ROWS = 208
GROUPS = 8
HALF = D // 2
HALF_FF = FF // 2
PAIR = 2 * HD
STEPS = 3
CHUNK = HALF_FF // STEPS
FEED = 2 * HALF_FF
ATTN = 4 * HALF
LAYER = FEED + ATTN
GATHERED = LAYER + ATTN
JOINED = LAYER + FEED
QUARTER = HALF_FF // 4
SIDE = 4
BLOCK = D // SIDE**2
MESH = ("section", "dp", "heads")
SWAP = [(0, 1), (1, 0)]
LIMIT = 48 * 2**20
ALL = 60 * 2**20
SCALE = HD ** (-0.5)
epsilon = 1e-06
f32 = jnp.float32
low = jnp.bfloat16


def dot(left, right):
    return jnp.dot(left, right, preferred_element_type=f32)


def dot_t(left, right):
    return lax.dot_general(left, right, (((1,), (1,)), ((), ())), preferred_element_type=f32)


def t_dot(left, right):
    return lax.dot_general(left, right, (((0,), (0,)), ((), ())), preferred_element_type=f32)


def both(own, other):
    return own[...].astype(f32) + other[...].astype(f32)


def column_sum(value):
    return jnp.sum(value.astype(f32), axis=0, keepdims=True)


def stats(value):
    average = jnp.mean(value, axis=-1, keepdims=True)
    centred = value - average
    rate = lax.rsqrt(jnp.mean(centred * centred, axis=-1, keepdims=True) + epsilon)
    return centred * rate, rate


def norm_back(value, gain, grad):
    x, rate = stats(value)
    scaled = grad * gain
    inner = scaled - jnp.mean(scaled, axis=-1, keepdims=True)
    inner = inner - x * jnp.mean(scaled * x, axis=-1, keepdims=True)
    return rate * inner, column_sum(grad * x), column_sum(grad)


def gauss(value):
    return 0.5 + 0.5 * lax.erf(value * 0.7071067811865476), jnp.exp(value * value * -0.5) * 0.3989422804014327


def head_masks():
    left = lax.broadcasted_iota(jnp.int32, (ROWS, PAIR), 1) < HD
    nothing = jnp.zeros((ROWS, PAIR), low)
    return left, (lambda rows: jnp.where(left, rows, nothing), lambda rows: jnp.where(left, nothing, rows))


def raw_scores(key_rows, queries):
    scores = dot_t(key_rows, queries) * SCALE
    return jnp.where(lax.broadcasted_iota(jnp.int32, scores.shape, 0) < PATCHES, scores, -1e30)


def start_blocks(slots, blocks, joined, sem, start, size, outwards=False):
    def body(inner, carry):
        for outer in range(SIDE):
            for half in range(2):
                i, j = (outer, inner) if outwards == (half == 0) else (inner, outer)
                row = pl.multiple_of(slots[i] * (SIDE * BLOCK) + slots[SIDE + j] * BLOCK, 16)
                ends = (
                    blocks[2 * half + outer // 2].at[outer % 2, inner, :, pl.ds(start, size)],
                    joined.at[pl.ds(row, BLOCK), pl.ds(half * size, size)],
                )
                pltpu.make_async_copy(*(reversed(ends) if outwards else ends), sem).start()
        return carry

    lax.fori_loop(0, SIDE, body, 0)


def all_landed(joined, sem):
    pltpu.make_async_copy(joined, joined, sem).wait()


def start_all(copies):
    for copy in copies:
        copy.start()


def wait_all(copies):
    for copy in copies:
        copy.wait()


def column_copies(whole, parts, sems, start, size, outwards=False):
    copies = []
    for k in range(parts.shape[0]):
        at = start[k] if isinstance(start, list) else start + k * size
        ends = whole.at[:, pl.ds(at, size)], parts.at[k]
        copies.append(pltpu.make_async_copy(*(reversed(ends) if outwards else ends), sems.at[k]))
    return copies


def column_copy(whole, parts, sems, start, size, k, outwards=False):
    ends = whole.at[:, pl.ds(pl.multiple_of(start + k * size, 128), size)], parts.at[k]
    return pltpu.make_async_copy(*(reversed(ends) if outwards else ends), sems.at[k])


def pair_forward(packed, write_lse):
    left, choose = head_masks()
    queries, keys, values = (packed[:, k * PAIR : (k + 1) * PAIR] for k in range(3))
    found = []
    for head in range(2):
        scores = raw_scores(keys, choose[head](queries))
        summit = jnp.max(scores, axis=0, keepdims=True)
        raised = jnp.exp(scores - summit)
        whole = jnp.sum(raised, axis=0, keepdims=True)
        write_lse(head, summit + jnp.log(whole))
        found.append(t_dot((raised * (1.0 / whole)).astype(low), values))
    return jnp.where(left, found[0], found[1]).astype(low)


def pair_backward(packed, lse, grad_pair, grad_packed):
    left, choose = head_masks()
    queries, keys, values = (packed[:, k * PAIR : (k + 1) * PAIR] for k in range(3))
    found = []
    for head in range(2):
        soft = jnp.exp(raw_scores(keys, choose[head](queries)) - lse[head : head + 1, :])
        grad_probs = dot_t(values, choose[head](grad_pair))
        within = jnp.sum(grad_probs * soft, axis=0, keepdims=True)
        grad_scores = (soft * (grad_probs - within)).astype(low)
        found.append((t_dot(grad_scores, keys) * SCALE, dot(grad_scores, queries) * SCALE, dot(soft.astype(low), grad_pair)))
    for k in range(3):
        grad_packed[:, k * PAIR : (k + 1) * PAIR] = jnp.where(left, found[0][k], found[1][k]).astype(low)
    return grad_packed[...]


def attention_kernel(second, *refs):
    if second:
        base, own, other, last_bias, norms, offset, weights, stream_out, *refs = refs
    else:
        base, norms, offset, weights, *refs = refs
    normed_out, packed_out, lse_out, context_out, part_out, weight, sems = refs
    copies = column_copies(weights, weight, sems, FEED + (ATTN if second else 0), 4 * PAIR)
    start_all(copies)
    stream = base[...]
    if second:
        stream = (stream + (both(own, other) + last_bias[...])).astype(low).astype(f32)
        stream_out[...] = stream
    normed = (stats(stream)[0] * norms[0:1] + norms[2:3]).astype(low)
    normed_out[...] = normed
    total = 0.0
    for k in range(STEPS):
        copies[k].wait()
        at = slice(k * 3 * PAIR, (k + 1) * 3 * PAIR)
        packed = (dot(normed, weight[k, :, : 3 * PAIR]) + offset[:, at]).astype(low)
        packed_out[:, at] = packed

        def write_lse(head, row):
            lse_out[k, head : head + 1, :] = row

        context = pair_forward(packed, write_lse)
        context_out[:, k * PAIR : (k + 1) * PAIR] = context
        total = total + dot_t(context, weight[k, :, 3 * PAIR :])
    part_out[...] = total.astype(low)


def forward_kernel(
    stream, own, other, norms, bias, weights, middle_out, normed_out, upper_out, part_out, weight, kept, sems, out_sems
):
    copies = column_copies(weights, weight, sems, 0, 2 * CHUNK)
    start_all(copies)
    leaving = column_copies(upper_out, kept, out_sems, 0, CHUNK, True)
    middle = stream[...] + (both(own, other) + norms[3:4])
    middle_out[...] = middle
    normed = (stats(middle)[0] * norms[1:2] + norms[4:5]).astype(low)
    normed_out[...] = normed
    total = 0.0
    for k in range(STEPS):
        copies[k].wait()
        upper = dot(normed, weight[k, :, :CHUNK]) + bias[:, k * CHUNK : (k + 1) * CHUNK]
        kept[k] = upper
        leaving[k].start()
        hidden = (upper * gauss(upper)[0]).astype(low)
        total = total + dot_t(hidden, weight[k, :, CHUNK:])
    part_out[...] = total.astype(low)
    for copy in leaving:
        copy.wait()


def turn_kernel(
    slots, branch, stream, own, other, norms, bias, near, far,
    grads_out, middle_out, mixed_out, part_out, bias_out, rows_out, weight, grads, normed, total, mixed, sems, out_sems,
):
    for k in range(SIDE):
        start_blocks(slots, [(near, far)[k // 2].at[k % 2, p] for p in range(SIDE)], weight.at[k], sems.at[k], 0, QUARTER)
    middle = stream[...] + (both(own, other) + norms[3:4])
    middle_out[...] = middle
    normed[...] = (stats(middle)[0] * norms[1:2] + norms[4:5]).astype(low)
    rows_out[2:3] = column_sum(branch[...])
    total[...] = jnp.zeros_like(total)
    mixed[...] = jnp.zeros_like(mixed)

    def leaving(k):
        columns = pl.ds(pl.multiple_of(slots[2 * SIDE + k] * 2 * QUARTER, 256), 2 * QUARTER)
        return pltpu.make_async_copy(grads.at[k], grads_out.at[:, columns], out_sems.at[k])

    def body(k, carry):
        at = pl.ds(pl.multiple_of(slots[2 * SIDE + k] * QUARTER, 128), QUARTER)
        rows, normed_now = branch[...], normed[...]
        all_landed(weight.at[k], sems.at[k])
        upper = dot(normed_now, weight[k, :, :QUARTER]) + bias[:, at]
        share, density = gauss(upper)
        hidden = (upper * share).astype(low)
        grad_upper = (dot(rows, weight[k, :, QUARTER:]) * (share + upper * density)).astype(low)
        total[...] += dot_t(grad_upper, weight[k, :, :QUARTER])
        grads[k, :, :QUARTER] = t_dot(normed_now, grad_upper).astype(low)
        grads[k, :, QUARTER:] = t_dot(rows, hidden).astype(low)
        leaving(k).start()
        bias_out[:, at] = column_sum(grad_upper)
        mixed[...] += dot_t(hidden, weight[k, :, QUARTER:])
        return carry

    lax.fori_loop(0, SIDE, body, 0)
    part_out[...] = total[...].astype(low)
    mixed_out[...] = mixed[...].astype(low)
    for k in range(SIDE):
        leaving(k).wait()


def backward_kernel(
    grad, own, other, stream, gains, normed_in, uppers, weights, _,
    grads_out, part_out, bias_out, rows_out, branch, weight, upper, grads, sems, upper_sems, out_sems,
):
    copies = column_copies(weights, weight, sems, 0, 2 * CHUNK)
    entering = column_copies(uppers, upper, upper_sems, 0, CHUNK)
    for pair in zip(copies, entering):
        for copy in pair:
            copy.start()
    leaving = column_copies(grads_out, grads, out_sems, FEED, 2 * CHUNK, True)
    into, gain, shift = norm_back(stream[...], gains[0:1], both(own, other))
    rows = (grad[...] + into).astype(low)
    branch[...] = rows
    rows_out[0:1] = gain
    rows_out[1:2] = shift
    rows_out[2:3] = column_sum(rows)
    normed = normed_in[...]

    def body(k, total):
        column_copy(uppers, upper, upper_sems, 0, CHUNK, k).wait()
        column_copy(weights, weight, sems, 0, 2 * CHUNK, k).wait()
        upper_now = upper[k]
        share, density = gauss(upper_now)
        hidden = (upper_now * share).astype(low)
        grad_upper = (dot(rows, weight[k, :, CHUNK:]) * (share + upper_now * density)).astype(low)
        grads[k, :, :CHUNK] = t_dot(normed, grad_upper).astype(low)
        grads[k, :, CHUNK:] = t_dot(rows, hidden).astype(low)
        column_copy(grads_out, grads, out_sems, FEED, 2 * CHUNK, k, True).start()
        bias_out[:, pl.ds(pl.multiple_of(k * CHUNK, 128), CHUNK)] = column_sum(grad_upper)
        return total + dot_t(grad_upper, weight[k, :, :CHUNK])

    part_out[...] = lax.fori_loop(0, STEPS, body, jnp.zeros((ROWS, D), f32)).astype(low)
    for copy in leaving:
        copy.wait()


def attention_back_kernel(second, *refs):
    if not second:
        slots, *refs = refs
    branch, own, other, middle, norms, normed_in, packed, lse, context, weights, *refs = refs
    if second:
        _, grads_out, *refs = refs
    else:
        blocks, refs = refs[:SIDE], refs[SIDE:]
    middle_out, part_out, rows_out, packed_out, weight, grads, grad_packed, sems, out_sems = refs
    copies = column_copies(weights, weight, sems, FEED + (ATTN if second else 0), 4 * PAIR)
    start_all(copies)
    if second:
        leaving = column_copies(grads_out, grads, out_sems, 2 * FEED, 4 * PAIR, True)
    into, gain, shift = norm_back(middle[...], norms[1:2], both(own, other))
    grad_middle = branch[...].astype(f32) + into
    middle_out[...] = grad_middle
    attn = grad_middle.astype(low)
    rows_out[0:1] = gain
    rows_out[1:2] = shift
    rows_out[2:3] = column_sum(attn)
    normed = normed_in[...]

    def pair_step(k, total):
        here, at = pl.ds(pl.multiple_of(k * PAIR, PAIR), PAIR), pl.ds(pl.multiple_of(k * 3 * PAIR, PAIR), 3 * PAIR)
        grad_pair = dot(attn, weight[k, :, 3 * PAIR :]).astype(low)
        rows = pair_backward(packed[:, at], lse[k], grad_pair, grad_packed)
        grads[k, :, : 3 * PAIR] = t_dot(normed, rows).astype(low)
        grads[k, :, 3 * PAIR :] = t_dot(attn, context[:, here]).astype(low)
        packed_out[:, at] = column_sum(rows)
        return total + dot_t(rows, weight[k, :, : 3 * PAIR])

    def body(k, total):
        column_copy(weights, weight, sems, FEED + (ATTN if second else 0), 4 * PAIR, k).wait()
        total = pair_step(k, total)
        if second:
            column_copy(grads_out, grads, out_sems, 2 * FEED, 4 * PAIR, k, True).start()
        else:
            start_blocks(slots, blocks, grads.at[k], out_sems.at[k], pl.multiple_of(2 * k * PAIR, 2 * PAIR), 2 * PAIR, True)
        return total

    total = lax.fori_loop(0, STEPS, body, jnp.zeros((ROWS, D), f32))
    part_out[...] = total.astype(low)
    for k in range(STEPS):
        if second:
            leaving[k].wait()
        else:
            all_landed(grads.at[k], out_sems.at[k])


def last_kernel(
    core, grad_middle, own, other, stream, norms, masked, tag, middle, mixed, mixed_other, last_bias,
    rows_one, sums_one, turn_rows, bias_one, rows_zero, sums_zero, back_rows, bias_zero, rows_out, vectors_low_out, vectors_out,
):
    into, gain, shift = norm_back(stream[...], norms[0:1], both(own, other))
    grad_zero = grad_middle[...] + into
    hidden = masked[...] > 0.5
    final = middle[...] + (both(mixed, mixed_other) + last_bias[...])
    first = core[0] == 0
    rows_out[...] = jnp.where(first, jnp.where(hidden, 0.0, grad_zero), final).astype(low)
    for at, gain_one, shift_one, attn_rows, feed_rows, sums, bias in (
        (0, gain, shift, rows_zero, back_rows, sums_zero, bias_zero),
        (9, back_rows[0:1], back_rows[1:2], rows_one, turn_rows, sums_one, bias_one),
    ):
        for k, row in enumerate((gain_one, attn_rows[0:1], shift_one, attn_rows[2:3], attn_rows[1:2], feed_rows[2:3])):
            vectors_out[at + k : at + k + 1] = row
        for k in range(STEPS):
            for part in range(2):
                to = part * HALF + k * PAIR
                vectors_out[at + 6 : at + 7, to : to + PAIR] = sums[:, (3 * k + 2 * part) * PAIR : (3 * k + 2 * part + 1) * PAIR]
        for k in range(2):
            vectors_out[at + 7 + k : at + 8 + k] = bias[:, k * D : (k + 1) * D]
    vectors_out[18:19] = column_sum(jnp.where(hidden, grad_zero, 0.0))
    table = column_sum(grad_zero)
    for group in range(GROUPS):
        vectors_out[19 + group : 20 + group] = jnp.where(tag[0] == group, table, 0.0)
    vectors_out[27:32] = jnp.zeros((5, D), f32)
    vectors_low_out[...] = jnp.zeros((BLOCK, 2 * HALF), low)
    vectors_low_out[0:32, 0:D] = vectors_out[...].astype(low)


def ends_kernel(order, parts, out):
    for k in range(SIDE):
        out[k * PATCHES : (k + 1) * PATCHES] = parts[order[k]].astype(f32)[:PATCHES]


def feed_columns(layer):
    size = QUARTER if layer == 1 else CHUNK
    return [(2 * at, slice(at, at + size), size) for at in range(0, HALF_FF, size)]


def attn_columns():
    return [[FEED + (4 * k + c) * PAIR for c in range(4)] for k in range(STEPS)]


def shards_kernel(core, qkv, out, up, down, mine_out, sent_out):
    def fill(layer, half, target):
        for to, units, size in feed_columns(layer):
            units = slice(units.start + half * HALF_FF, units.stop + half * HALF_FF)
            target[:, to : to + size] = up[:, units].astype(low)
            target[:, to + size : to + 2 * size] = down[:, units].astype(low)
        for k, spots in enumerate(attn_columns()):
            at = slice(half * HALF + k * PAIR, half * HALF + (k + 1) * PAIR)
            for to, rows in zip(spots, (qkv[0, :, at], qkv[1, :, at], qkv[2, :, at], out[:, at])):
                target[:, to : to + PAIR] = rows.astype(low)

    for index in range(2):
        @pl.when(core[0] == index)
        def _():
            fill(index, index, mine_out)
            fill(index, 1 - index, sent_out)


def grads_kernel(
    core, first_half, second_half,
    qkv_out, out_out, up_out, down_out, qv_out, hidden_out, gains_out, biases_out, token_out, table_out,
):
    halves = first_half, second_half
    shared = first_half[:, LAYER : LAYER + D].astype(f32)

    def fill(layer, half, part):
        for at, units, size in feed_columns(layer):
            units = slice(units.start + half * HALF_FF, units.stop + half * HALF_FF)
            up_out[:, units] = part[:, at : at + size].astype(f32)
            down_out[:, units] = part[:, at + size : at + 2 * size].astype(f32)
        for k, spots in enumerate(attn_columns()):
            to = slice(half * HALF + k * PAIR, half * HALF + (k + 1) * PAIR)
            for c in range(3):
                qkv_out[c, :, to] = part[:, spots[c] : spots[c] + PAIR].astype(f32)
            out_out[:, to] = part[:, spots[3] : spots[3] + PAIR].astype(f32)

    for index in range(2):
        @pl.when(core[0] == index)
        def _():
            at = 9 * index
            gains_out[...] = shared[at : at + 2]
            biases_out[...] = shared[at + 2 : at + 6]
            token_out[...] = shared[18:19, index * HALF : (index + 1) * HALF]
            table_out[...] = shared[19 : 19 + GROUPS, index * HALF : (index + 1) * HALF]
            for h, half in enumerate(halves):
                fill(index, h, half)
                rows = half[:, LAYER : LAYER + D].astype(f32)
                for k in range(2):
                    qv_out[k : k + 1, h * HALF : (h + 1) * HALF] = rows[at + 6 : at + 7, k * HALF : (k + 1) * HALF]
                    hidden_out[:, h * HALF_FF + k * D : h * HALF_FF + (k + 1) * D] = rows[at + 7 + k : at + 8 + k]


def whole(array):
    return pl.BlockSpec(array.shape, lambda *_: (0,) * len(array.shape))


def shaped(shape, kind=f32):
    return jax.ShapeDtypeStruct(shape, kind)


def call(kernel, name, operands, outs, specs, micros, alias=None, scratch=(), limit=LIMIT):
    def spec(key, array):
        return specs.get(key) or whole(array)

    return pl.pallas_call(
        kernel,
        name=name,
        grid=(1,),
        in_specs=[spec(("in", k), a) for k, a in enumerate(operands)],
        out_specs=[spec(("out", k), a) for k, a in enumerate(outs)],
        out_shape=outs,
        scratch_shapes=scratch,
        input_output_aliases=alias or {},
        cost_estimate=pl.CostEstimate(flops=0, bytes_accessed=int(micros * 3.6e6), transcendentals=0),
        compiler_params=pltpu.CompilerParams(vmem_limit_bytes=limit),
    )(*operands)


SMALL = pl.BlockSpec(memory_space=pltpu.SMEM)
LEFT = pl.BlockSpec(memory_space=pl.ANY)


STREAM = shaped((ROWS, D))
STREAM_LOW = shaped((ROWS, D), low)


DMA = pltpu.SemaphoreType.DMA((STEPS,))
FEED_PARTS = pltpu.VMEM((STEPS, D, 2 * CHUNK), low)
ATTN_PARTS = pltpu.VMEM((STEPS, D, 4 * PAIR), low)
UPPER_PARTS = pltpu.VMEM((STEPS, ROWS, CHUNK), f32)
ATTN_KEPT = [STREAM_LOW, shaped((ROWS, 3 * HALF), low), shaped((STEPS, 8, ROWS)), shaped((ROWS, HALF), low), STREAM_LOW]
JOINED_GRADS = shaped((D, JOINED), low)


def attention_call(layer, entry, norms, offset, weights):
    second = layer == 1
    operands = (*entry, norms, offset, weights)
    return call(
        functools.partial(attention_kernel, second), f"attention_{layer}", operands, [STREAM, *ATTN_KEPT] if second else ATTN_KEPT,
        {("in", len(operands) - 1): LEFT}, 4, scratch=[ATTN_PARTS, DMA],
    )


def forward_call(stream, part, part_other, norms, bias_up, weights):
    return call(
        forward_kernel, "feed_0", (stream, part, part_other, norms, bias_up, weights),
        [STREAM, STREAM_LOW, shaped((ROWS, HALF_FF)), STREAM_LOW], {("in", 5): LEFT, ("out", 2): LEFT}, 4,
        scratch=[FEED_PARTS, UPPER_PARTS, DMA, DMA],
    )


def turn_call(slots, branch, stream, part, part_other, norms, bias_up, near, far):
    parts, sems = pltpu.VMEM((SIDE, D, 2 * QUARTER), low), pltpu.SemaphoreType.DMA((SIDE,))
    return call(
        turn_kernel, "feed_1", (slots, branch, stream, part, part_other, norms, bias_up, near, far),
        [JOINED_GRADS, STREAM, STREAM_LOW, STREAM_LOW, shaped((1, HALF_FF)), shaped((8, D))],
        {("in", 0): SMALL, ("in", 7): LEFT, ("in", 8): LEFT, ("out", 0): LEFT}, 9,
        scratch=[parts, parts, pltpu.VMEM((ROWS, D), low), *[pltpu.VMEM((ROWS, D), f32)] * 2, sems, sems],
    )


def backward_call(entry, normed, upper, weights, grads):
    return call(
        backward_kernel, "feed_back_0", (*entry, normed, upper, weights, grads),
        [JOINED_GRADS, STREAM_LOW, shaped((1, HALF_FF)), shaped((8, D)), STREAM_LOW],
        {("in", 6): LEFT, ("in", 7): LEFT, ("in", 8): LEFT, ("out", 0): LEFT}, 6, alias={8: 0},
        scratch=[FEED_PARTS, UPPER_PARTS, FEED_PARTS, DMA, DMA, DMA],
    )


def attention_back_call(layer, entry, branch, part, part_other, middle, norms, normed, packed, lse, context, weights, grads):
    second = layer == 1
    operands = (*entry, branch, part, part_other, middle, norms, normed, packed, lse, context, weights, *grads)
    outs = [JOINED_GRADS] if second else [shaped((2, SIDE, BLOCK, 2 * HALF), low)] * SIDE
    count, last = len(outs), len(operands) - 1
    specs = {("in", k): LEFT for k in ((last - 1, last) if second else (last,))}
    if not second:
        specs["in", 0] = SMALL
    specs.update({("out", k): LEFT for k in range(count)})
    made = call(
        functools.partial(attention_back_kernel, second), f"attention_back_{layer}", operands,
        [*outs, STREAM, STREAM_LOW, shaped((8, D)), shaped((1, 3 * HALF))], specs, 7, alias={last: 0} if second else None,
        scratch=[ATTN_PARTS, ATTN_PARTS, pltpu.VMEM((ROWS, 3 * PAIR), low), DMA, DMA],
    )
    return made[:count], made[count:]


def swap(value):
    return lax.ppermute(value, "section", SWAP)


def routes(axis, turn):
    pairs = []
    for place in range(2 * SIDE**3):
        spot = [place // SIDE**3, place // SIDE**2 % SIDE, place // SIDE % SIDE, place % SIDE]
        spot[axis + 1] ^= 1 if spot[0] == turn else 3
        pairs.append((place, ((spot[0] * SIDE + spot[1]) * SIDE + spot[2]) * SIDE + spot[3]))
    return pairs


def trade(value, axis, turn):
    return lax.ppermute(value, MESH, routes(axis, turn))


def add(*values):
    return functools.reduce(jnp.add, (v.astype(f32) for v in values)).astype(low)


def both_of(own, axis, turn):
    return jnp.stack([own, trade(own, axis, turn)])


def gather_first(own, axis):
    pair = both_of(own, axis, 0)
    return jnp.concatenate([pair, trade(pair, axis, 1)])


def gather_second(own, axis):
    pair = both_of(own, axis, 0)
    return pair, trade(pair, axis, 1)


def halves_of(kept, got):
    middle = kept.shape[0] // 2
    return add(kept[:middle], got[:middle]), add(kept[middle:], got[middle:])


tied = lax.optimization_barrier


def per_device(
    patches, mask_flags, image_tags, mask_token, group_table, qkv_weight, query_value_bias, out_weight,
    up_weight, hidden_bias, down_weight, norm_gains, norm_biases, cotangent,
):
    place = lax.axis_index("heads")
    core = lax.axis_index("section")
    first = core == 0

    x, y = lax.axis_index("dp") // SIDE, lax.axis_index("dp") % SIDE
    flips = jnp.where(first, jnp.array([0, 1, 3, 2], jnp.int32), jnp.array([0, 3, 1, 2], jnp.int32))
    slots = jnp.concatenate([x ^ flips, y ^ flips, place ^ flips])
    order = jnp.argmax((place ^ flips)[None, :] == jnp.arange(SIDE, dtype=jnp.int32)[:, None], axis=1).astype(jnp.int32)

    rows = qkv_weight.shape[1]
    mine, other = call(
        shards_kernel, "shards",
        (core.reshape(1), qkv_weight[0].transpose(1, 0, 2), out_weight[0].T, up_weight[0], down_weight[0].T),
        [shaped((rows, LAYER), low)] * 2, {("in", 0): SMALL}, 2, limit=ALL,
    )
    other = swap(other)
    zero, one = jnp.where(first, mine, other), jnp.where(first, other, mine)

    shard = jnp.concatenate([zero, one[:, FEED:]], axis=1)
    weights = lax.all_gather(shard, "dp", axis=0, tiled=True)
    quarter = lax.dynamic_slice_in_dim(one, place * 2 * QUARTER, 2 * QUARTER, 1)
    near = gather_first(quarter[:, :QUARTER], 0), gather_first(quarter[:, QUARTER:], 1)
    near = jnp.stack([*gather_second(near[0], 1), *gather_second(near[1], 0)])
    near = both_of(near, 2, 0)
    far = trade(near, 2, 1)
    later = (patches, mask_flags, image_tags, mask_token, group_table, cotangent, norm_gains, norm_biases, query_value_bias, hidden_bias)
    later, _ = tied((later, near))
    patches, mask_flags, image_tags, mask_token, group_table, cotangent, norm_gains, norm_biases, query_value_bias, hidden_bias = later

    def half_of(vector):
        return jnp.where(first, vector[..., : vector.shape[-1] // 2], vector[..., vector.shape[-1] // 2 :])

    vectors = lax.all_gather(
        jnp.concatenate([norm_gains[0], norm_biases[0], query_value_bias[0], hidden_bias[0].reshape(4, D)]),
        "section", axis=0,
    )
    norms, offsets, bias_ups = [], [], []
    for layer in range(2):
        v = vectors[layer]
        norms.append(jnp.pad(v[:6], ((0, 2), (0, 0))))
        query, value = half_of(v[6:8]).reshape(2, STEPS, PAIR)
        offsets.append(jnp.stack([query, jnp.zeros_like(query), value], axis=1).reshape(1, 3 * HALF))
        bias_ups.append(half_of(v[8:12].reshape(1, FF)))

    def own(rows_of):
        return lax.dynamic_slice_in_dim(rows_of, place * PATCHES, PATCHES, 0)

    def padded(value):
        return jnp.pad(value, ((0, ROWS - PATCHES), (0, 0)))

    masked = lax.dynamic_slice_in_dim(mask_flags, place, 1, 0).reshape(PATCHES, 1).astype(f32)
    tag = lax.dynamic_slice_in_dim(image_tags, place, 1, 0)
    onehot = (tag[:, None] == jnp.arange(GROUPS, dtype=jnp.int32)[None, :]).astype(f32)
    image_row = jnp.sum(onehot.T * group_table, axis=0, keepdims=True)
    stream_zero = padded(jnp.where(masked > 0, mask_token[None, :], own(patches).astype(f32)) + image_row)
    seed, masked = padded(own(cotangent)), padded(masked)

    normed, packed, lse, context, part = attention_call(0, (stream_zero,), norms[0], offsets[0], weights)
    middle, normed_two, upper, mixed = forward_call(stream_zero, part, swap(part), norms[0], bias_ups[0], weights)
    kept = (middle, norms[0], normed, packed, lse, context)
    stream_one, normed, packed, lse, context, part = attention_call(
        1, (middle, mixed, swap(mixed), norms[0][5:6]), norms[1], offsets[1], weights
    )
    grads, middle, mixed, part, bias_one, turn_rows = turn_call(
        slots, seed, stream_one, part, swap(part), norms[1], bias_ups[1], near, far
    )
    (grads,), (grad_middle, part, rows_one, sums_one) = attention_back_call(
        1, (), seed, part, swap(part), middle, norms[1], normed, packed, lse, context, weights, [grads]
    )
    grads, part, bias_zero, back_rows, branch = backward_call(
        (grad_middle, part, swap(part), stream_one, norms[1]), normed_two, upper, weights, grads
    )
    joined = lax.psum_scatter(grads, "dp", scatter_dimension=0, tiled=True)
    (zero, sent, zero_too, sent_too), (grad_middle, part, rows_zero, sums_zero) = attention_back_call(
        0, (slots,), branch, part, swap(part), *kept, weights, []
    )
    rows_out, vectors, _ = call(
        last_kernel, "last",
        (
            core.reshape(1), grad_middle, part, swap(part), stream_zero, norms[0], masked, tag, middle, mixed, swap(mixed),
            norms[1][5:6], rows_one, sums_one, turn_rows, bias_one, rows_zero, sums_zero, back_rows, bias_zero,
        ),
        [STREAM_LOW, shaped((BLOCK, D), low), shaped((32, D))], {("in", 0): SMALL, ("in", 7): SMALL}, 3, limit=ALL,
    )

    def trade_with(sent, vectors, axis, turn):
        got = trade(jnp.concatenate([sent.reshape(-1, BLOCK, D), vectors[None]]), axis, turn)
        return got[:-1].reshape(sent.shape), add(vectors, got[-1])

    (got, vectors), got_too = trade_with(sent, vectors, 0, 1), trade(sent_too, 1, 1)
    got, got_too, rows_out = tied((got, got_too, rows_out))
    ends = both_of(rows_out, 2, 0)
    (zero, sent), (zero_too, sent_too) = halves_of(zero, got), halves_of(zero_too, got_too)
    (got, vectors), got_too = trade_with(sent, vectors, 0, 0), trade(sent_too, 1, 0)
    got, got_too, ends = tied((got, got_too, ends))
    ends = jnp.concatenate([ends, trade(ends, 2, 1)])
    (zero, sent), (zero_too, sent_too) = halves_of(zero[0], got[0]), halves_of(zero_too[0], got_too[0])
    (got, vectors), got_too = trade_with(sent, vectors, 1, 1), trade(sent_too, 0, 1)
    (zero, sent), (zero_too, sent_too) = halves_of(zero, got), halves_of(zero_too, got_too)
    (got, vectors), got_too = trade_with(sent, vectors, 1, 0), trade(sent_too, 0, 0)
    def by_pair(wide):
        return [wide[:, s * 2 * HALF + k * 2 * PAIR : s * 2 * HALF + (k + 1) * 2 * PAIR] for k in range(STEPS) for s in (0, 1)]

    attn_sum = jnp.concatenate([*by_pair(jnp.concatenate([add(zero[0], got[0]), add(zero_too[0], got_too[0])], axis=1)), vectors], axis=1)

    def z_sum(value):
        value = add(value, trade(value, 2, 0))
        return add(value, trade(value, 2, 1))

    attn_sum = z_sum(attn_sum)
    (ends_here,) = call(
        ends_kernel, "ends", (order, ends), [shaped((SIDE * PATCHES, D))], {("in", 0): SMALL}, 2
    )
    joined, attn_sum, ends_here = tied((joined, attn_sum, ends_here))

    joined = z_sum(joined)
    zero = jnp.concatenate([joined[:, FEED : 2 * FEED], attn_sum], axis=1)
    one = jnp.concatenate([joined[:, :FEED], joined[:, 2 * FEED :], attn_sum[:, ATTN:]], axis=1)
    mine = jnp.where(first, zero, one)
    other = swap(jnp.where(first, one, zero))
    grad_qkv, grad_out, grad_up, grad_down, grad_qv, grad_hidden, grad_gains, grad_biases, grad_token, grad_table = call(
        grads_kernel, "grads", (core.reshape(1), jnp.where(first, mine, other), jnp.where(first, other, mine)),
        [
            shaped((3, rows, D)), shaped((rows, D)), shaped((rows, FF)), shaped((rows, FF)), shaped((2, D)), shaped((1, FF)),
            shaped((2, D)), shaped((4, D)), shaped((1, HALF)), shaped((GROUPS, HALF)),
        ],
        {("in", 0): SMALL}, 2,
    )
    return (
        ends_here[None], grad_qkv.transpose(1, 0, 2)[None], grad_qv[None], grad_out.T[None], grad_up[None], grad_hidden,
        grad_down.T[None], grad_gains[None], grad_biases[None], grad_token[0], grad_table,
    )


def solution(mesh):
    in_specs = (
        P("dp", None), P("dp", None), P("dp"), P(), P(),
        P("section", "dp", None, None), P("section", None, None), P("section", None, "dp"),
        P("section", "dp", None), P("section", None), P("section", None, "dp"),
        P("section", None, None), P("section", None, None), P("dp", None),
    )
    out_specs = (
        P("section", "dp", None), P("section", "dp", None, None), P("section", None, None),
        P("section", None, "dp"), P("section", "dp", None), P("section", None), P("section", None, "dp"),
        P("section", None, None), P("section", None, None), P("section"), P(None, "section"),
    )
    return jax.shard_map(per_device, mesh=mesh, in_specs=in_specs, out_specs=out_specs, check_vma=False)
```

```python
import functools

import jax
import jax.numpy as jnp
from jax import lax
from jax.experimental import pallas as pl
from jax.experimental.pallas import tpu as pltpu
from jax.sharding import PartitionSpec as P

D = 768
HD = 64
FF = 3072
PATCHES = 196
ROWS = 208
GROUPS = 8
HALF = D // 2
HALF_FF = FF // 2
PAIR = 2 * HD
STEPS = 3
CHUNK = HALF_FF // STEPS
FEED = 2 * HALF_FF
ATTN = 4 * HALF
LAYER = FEED + ATTN
GATHERED = LAYER + ATTN
JOINED = LAYER + FEED
QUARTER = HALF_FF // 4
SIDE = 4
BLOCK = D // SIDE**2
MESH = ("section", "dp", "heads")
SWAP = [(0, 1), (1, 0)]
LIMIT = 48 * 2**20
ALL = 60 * 2**20
SCALE = HD ** (-0.5)
epsilon = 1e-06
f32 = jnp.float32
low = jnp.bfloat16


def dot(left, right):
    return jnp.dot(left, right, preferred_element_type=f32)


def dot_t(left, right):
    return lax.dot_general(left, right, (((1,), (1,)), ((), ())), preferred_element_type=f32)


def t_dot(left, right):
    return lax.dot_general(left, right, (((0,), (0,)), ((), ())), preferred_element_type=f32)


def both(own, other):
    return own[...].astype(f32) + other[...].astype(f32)


def column_sum(value):
    return jnp.sum(value.astype(f32), axis=0, keepdims=True)


def stats(value):
    average = jnp.mean(value, axis=-1, keepdims=True)
    centred = value - average
    rate = lax.rsqrt(jnp.mean(centred * centred, axis=-1, keepdims=True) + epsilon)
    return centred * rate, rate


def norm_back(value, gain, grad):
    x, rate = stats(value)
    scaled = grad * gain
    inner = scaled - jnp.mean(scaled, axis=-1, keepdims=True)
    inner = inner - x * jnp.mean(scaled * x, axis=-1, keepdims=True)
    return rate * inner, column_sum(grad * x), column_sum(grad)


def gauss(value):
    return 0.5 + 0.5 * lax.erf(value * 0.7071067811865476), jnp.exp(value * value * -0.5) * 0.3989422804014327


def head_masks():
    left = lax.broadcasted_iota(jnp.int32, (ROWS, PAIR), 1) < HD
    nothing = jnp.zeros((ROWS, PAIR), low)
    return left, (lambda rows: jnp.where(left, rows, nothing), lambda rows: jnp.where(left, nothing, rows))


def raw_scores(key_rows, queries):
    scores = dot_t(key_rows, queries) * SCALE
    return jnp.where(lax.broadcasted_iota(jnp.int32, scores.shape, 0) < PATCHES, scores, -1e30)


def start_blocks(slots, blocks, joined, sem, start, size, outwards=False):
    def body(inner, carry):
        for outer in range(SIDE):
            for half in range(2):
                i, j = (outer, inner) if outwards == (half == 0) else (inner, outer)
                row = pl.multiple_of(slots[i] * (SIDE * BLOCK) + slots[SIDE + j] * BLOCK, 16)
                ends = (
                    blocks[2 * half + outer // 2].at[outer % 2, inner, :, pl.ds(start, size)],
                    joined.at[pl.ds(row, BLOCK), pl.ds(half * size, size)],
                )
                pltpu.make_async_copy(*(reversed(ends) if outwards else ends), sem).start()
        return carry

    lax.fori_loop(0, SIDE, body, 0)


def start_kinds(slots, outs, joined, sem, start):
    def body(j, carry):
        for k in range(SIDE):
            kind = pl.ds(pl.multiple_of(slots[2 * SIDE + k] * PAIR, PAIR), PAIR)
            for i in range(SIDE):
                row = pl.multiple_of(slots[i] * (SIDE * BLOCK) + slots[SIDE + j] * BLOCK, 16)
                there = outs[k // 2].at[k % 2, i // 2, i % 2, j, :, pl.ds(start, PAIR)]
                pltpu.make_async_copy(joined.at[pl.ds(row, BLOCK), kind], there, sem).start()
        return carry

    lax.fori_loop(0, SIDE, body, 0)


def all_landed(joined, sem):
    pltpu.make_async_copy(joined, joined, sem).wait()


def start_all(copies):
    for copy in copies:
        copy.start()


def wait_all(copies):
    for copy in copies:
        copy.wait()


def column_copies(whole, parts, sems, start, size, outwards=False):
    copies = []
    for k in range(parts.shape[0]):
        at = start[k] if isinstance(start, list) else start + k * size
        ends = whole.at[:, pl.ds(at, size)], parts.at[k]
        copies.append(pltpu.make_async_copy(*(reversed(ends) if outwards else ends), sems.at[k]))
    return copies


def column_copy(whole, parts, sems, start, size, k, outwards=False):
    ends = whole.at[:, pl.ds(pl.multiple_of(start + k * size, 128), size)], parts.at[k]
    return pltpu.make_async_copy(*(reversed(ends) if outwards else ends), sems.at[k])


def pair_forward(packed, write_lse):
    left, choose = head_masks()
    queries, keys, values = (packed[:, k * PAIR : (k + 1) * PAIR] for k in range(3))
    found = []
    for head in range(2):
        scores = raw_scores(keys, choose[head](queries))
        summit = jnp.max(scores, axis=0, keepdims=True)
        raised = jnp.exp(scores - summit)
        whole = jnp.sum(raised, axis=0, keepdims=True)
        write_lse(head, summit + jnp.log(whole))
        found.append(t_dot((raised * (1.0 / whole)).astype(low), values))
    return jnp.where(left, found[0], found[1]).astype(low)


def pair_backward(packed, lse, grad_pair, grad_packed):
    left, choose = head_masks()
    queries, keys, values = (packed[:, k * PAIR : (k + 1) * PAIR] for k in range(3))
    found = []
    for head in range(2):
        soft = jnp.exp(raw_scores(keys, choose[head](queries)) - lse[head : head + 1, :])
        grad_probs = dot_t(values, choose[head](grad_pair))
        within = jnp.sum(grad_probs * soft, axis=0, keepdims=True)
        grad_scores = (soft * (grad_probs - within)).astype(low)
        found.append((t_dot(grad_scores, keys) * SCALE, dot(grad_scores, queries) * SCALE, dot(soft.astype(low), grad_pair)))
    for k in range(3):
        grad_packed[:, k * PAIR : (k + 1) * PAIR] = jnp.where(left, found[0][k], found[1][k]).astype(low)
    return grad_packed[...]


def attention_kernel(second, *refs):
    if second:
        base, own, other, last_bias, norms, offset, weights, stream_out, *refs = refs
    else:
        base, norms, offset, weights, *refs = refs
    normed_out, packed_out, lse_out, context_out, part_out, weight, sems = refs
    copies = column_copies(weights, weight, sems, FEED + (ATTN if second else 0), 4 * PAIR)
    start_all(copies)
    stream = base[...]
    if second:
        stream = (stream + (both(own, other) + last_bias[...])).astype(low).astype(f32)
        stream_out[...] = stream
    normed = (stats(stream)[0] * norms[0:1] + norms[2:3]).astype(low)
    normed_out[...] = normed
    total = 0.0
    for k in range(STEPS):
        copies[k].wait()
        at = slice(k * 3 * PAIR, (k + 1) * 3 * PAIR)
        packed = (dot(normed, weight[k, :, : 3 * PAIR]) + offset[:, at]).astype(low)
        packed_out[:, at] = packed

        def write_lse(head, row):
            lse_out[k, head : head + 1, :] = row

        context = pair_forward(packed, write_lse)
        context_out[:, k * PAIR : (k + 1) * PAIR] = context
        total = total + dot_t(context, weight[k, :, 3 * PAIR :])
    part_out[...] = total.astype(low)


def forward_kernel(
    stream, own, other, norms, bias, weights, middle_out, normed_out, upper_out, part_out, weight, kept, sems, out_sems
):
    copies = column_copies(weights, weight, sems, 0, 2 * CHUNK)
    start_all(copies)
    leaving = column_copies(upper_out, kept, out_sems, 0, CHUNK, True)
    middle = stream[...] + (both(own, other) + norms[3:4])
    middle_out[...] = middle
    normed = (stats(middle)[0] * norms[1:2] + norms[4:5]).astype(low)
    normed_out[...] = normed
    total = 0.0
    for k in range(STEPS):
        copies[k].wait()
        upper = dot(normed, weight[k, :, :CHUNK]) + bias[:, k * CHUNK : (k + 1) * CHUNK]
        kept[k] = upper
        leaving[k].start()
        hidden = (upper * gauss(upper)[0]).astype(low)
        total = total + dot_t(hidden, weight[k, :, CHUNK:])
    part_out[...] = total.astype(low)
    for copy in leaving:
        copy.wait()


def turn_kernel(
    slots, branch, stream, own, other, norms, bias, near, far,
    grads_out, middle_out, mixed_out, part_out, bias_out, rows_out, weight, grads, normed, total, mixed, sems, out_sems,
):
    for k in range(SIDE):
        start_blocks(slots, [(near, far)[k // 2].at[k % 2, p] for p in range(SIDE)], weight.at[k], sems.at[k], 0, QUARTER)
    middle = stream[...] + (both(own, other) + norms[3:4])
    middle_out[...] = middle
    normed[...] = (stats(middle)[0] * norms[1:2] + norms[4:5]).astype(low)
    rows_out[2:3] = column_sum(branch[...])
    total[...] = jnp.zeros_like(total)
    mixed[...] = jnp.zeros_like(mixed)

    def leaving(k):
        columns = pl.ds(pl.multiple_of(slots[2 * SIDE + k] * 2 * QUARTER, 256), 2 * QUARTER)
        return pltpu.make_async_copy(grads.at[k], grads_out.at[:, columns], out_sems.at[k])

    def body(k, carry):
        at = pl.ds(pl.multiple_of(slots[2 * SIDE + k] * QUARTER, 128), QUARTER)
        rows, normed_now = branch[...], normed[...]
        all_landed(weight.at[k], sems.at[k])
        upper = dot(normed_now, weight[k, :, :QUARTER]) + bias[:, at]
        share, density = gauss(upper)
        hidden = (upper * share).astype(low)
        grad_upper = (dot(rows, weight[k, :, QUARTER:]) * (share + upper * density)).astype(low)
        total[...] += dot_t(grad_upper, weight[k, :, :QUARTER])
        grads[k, :, :QUARTER] = t_dot(normed_now, grad_upper).astype(low)
        grads[k, :, QUARTER:] = t_dot(rows, hidden).astype(low)
        leaving(k).start()
        bias_out[:, at] = column_sum(grad_upper)
        mixed[...] += dot_t(hidden, weight[k, :, QUARTER:])
        return carry

    lax.fori_loop(0, SIDE, body, 0)
    part_out[...] = total[...].astype(low)
    mixed_out[...] = mixed[...].astype(low)
    for k in range(SIDE):
        leaving(k).wait()


def backward_kernel(
    grad, own, other, stream, gains, normed_in, uppers, weights, _,
    grads_out, part_out, bias_out, rows_out, branch, weight, upper, grads, sems, upper_sems, out_sems,
):
    copies = column_copies(weights, weight, sems, 0, 2 * CHUNK)
    entering = column_copies(uppers, upper, upper_sems, 0, CHUNK)
    for pair in zip(copies, entering):
        for copy in pair:
            copy.start()
    leaving = column_copies(grads_out, grads, out_sems, FEED, 2 * CHUNK, True)
    into, gain, shift = norm_back(stream[...], gains[0:1], both(own, other))
    rows = (grad[...] + into).astype(low)
    branch[...] = rows
    rows_out[0:1] = gain
    rows_out[1:2] = shift
    rows_out[2:3] = column_sum(rows)
    normed = normed_in[...]

    def body(k, total):
        column_copy(uppers, upper, upper_sems, 0, CHUNK, k).wait()
        column_copy(weights, weight, sems, 0, 2 * CHUNK, k).wait()
        upper_now = upper[k]
        share, density = gauss(upper_now)
        hidden = (upper_now * share).astype(low)
        grad_upper = (dot(rows, weight[k, :, CHUNK:]) * (share + upper_now * density)).astype(low)
        grads[k, :, :CHUNK] = t_dot(normed, grad_upper).astype(low)
        grads[k, :, CHUNK:] = t_dot(rows, hidden).astype(low)
        column_copy(grads_out, grads, out_sems, FEED, 2 * CHUNK, k, True).start()
        bias_out[:, pl.ds(pl.multiple_of(k * CHUNK, 128), CHUNK)] = column_sum(grad_upper)
        return total + dot_t(grad_upper, weight[k, :, :CHUNK])

    part_out[...] = lax.fori_loop(0, STEPS, body, jnp.zeros((ROWS, D), f32)).astype(low)
    for copy in leaving:
        copy.wait()


def attention_back_kernel(second, *refs):
    if not second:
        slots, *refs = refs
    branch, own, other, middle, norms, normed_in, packed, lse, context, weights, *refs = refs
    if second:
        _, grads_out, *refs = refs
    else:
        kept_out, sent_out, *refs = refs
    middle_out, part_out, rows_out, packed_out, weight, grads, grad_packed, sems, out_sems = refs
    copies = column_copies(weights, weight, sems, FEED + (ATTN if second else 0), 4 * PAIR)
    start_all(copies)
    if second:
        leaving = column_copies(grads_out, grads, out_sems, 2 * FEED, 4 * PAIR, True)
    into, gain, shift = norm_back(middle[...], norms[1:2], both(own, other))
    grad_middle = branch[...].astype(f32) + into
    middle_out[...] = grad_middle
    attn = grad_middle.astype(low)
    rows_out[0:1] = gain
    rows_out[1:2] = shift
    rows_out[2:3] = column_sum(attn)
    normed = normed_in[...]

    def pair_step(k, total):
        here, at = pl.ds(pl.multiple_of(k * PAIR, PAIR), PAIR), pl.ds(pl.multiple_of(k * 3 * PAIR, PAIR), 3 * PAIR)
        grad_pair = dot(attn, weight[k, :, 3 * PAIR :]).astype(low)
        rows = pair_backward(packed[:, at], lse[k], grad_pair, grad_packed)
        grads[k, :, : 3 * PAIR] = t_dot(normed, rows).astype(low)
        grads[k, :, 3 * PAIR :] = t_dot(attn, context[:, here]).astype(low)
        packed_out[:, at] = column_sum(rows)
        return total + dot_t(rows, weight[k, :, : 3 * PAIR])

    def body(k, total):
        column_copy(weights, weight, sems, FEED + (ATTN if second else 0), 4 * PAIR, k).wait()
        total = pair_step(k, total)
        if second:
            column_copy(grads_out, grads, out_sems, 2 * FEED, 4 * PAIR, k, True).start()
        else:
            start_kinds(slots, (kept_out, sent_out), grads.at[k], out_sems.at[k], pl.multiple_of(k * PAIR, PAIR))
        return total

    total = lax.fori_loop(0, STEPS, body, jnp.zeros((ROWS, D), f32))
    part_out[...] = total.astype(low)
    for k in range(STEPS):
        if second:
            leaving[k].wait()
        else:
            all_landed(grads.at[k], out_sems.at[k])


def last_kernel(
    core, grad_middle, own, other, stream, norms, masked, tag, middle, mixed, mixed_other, last_bias,
    rows_one, sums_one, turn_rows, bias_one, rows_zero, sums_zero, back_rows, bias_zero, rows_out, vectors_low_out, vectors_out,
):
    into, gain, shift = norm_back(stream[...], norms[0:1], both(own, other))
    grad_zero = grad_middle[...] + into
    hidden = masked[...] > 0.5
    final = middle[...] + (both(mixed, mixed_other) + last_bias[...])
    first = core[0] == 0
    rows_out[...] = jnp.where(first, jnp.where(hidden, 0.0, grad_zero), final).astype(low)
    for at, gain_one, shift_one, attn_rows, feed_rows, sums, bias in (
        (0, gain, shift, rows_zero, back_rows, sums_zero, bias_zero),
        (9, back_rows[0:1], back_rows[1:2], rows_one, turn_rows, sums_one, bias_one),
    ):
        for k, row in enumerate((gain_one, attn_rows[0:1], shift_one, attn_rows[2:3], attn_rows[1:2], feed_rows[2:3])):
            vectors_out[at + k : at + k + 1] = row
        for k in range(STEPS):
            for part in range(2):
                to = part * HALF + k * PAIR
                vectors_out[at + 6 : at + 7, to : to + PAIR] = sums[:, (3 * k + 2 * part) * PAIR : (3 * k + 2 * part + 1) * PAIR]
        for k in range(2):
            vectors_out[at + 7 + k : at + 8 + k] = bias[:, k * D : (k + 1) * D]
    vectors_out[18:19] = column_sum(jnp.where(hidden, grad_zero, 0.0))
    table = column_sum(grad_zero)
    for group in range(GROUPS):
        vectors_out[19 + group : 20 + group] = jnp.where(tag[0] == group, table, 0.0)
    vectors_out[27:32] = jnp.zeros((5, D), f32)
    vectors_low_out[...] = jnp.zeros((BLOCK, 2 * HALF), low)
    vectors_low_out[0:32, 0:D] = vectors_out[...].astype(low)


def ends_kernel(order, parts, out):
    for k in range(SIDE):
        out[k * PATCHES : (k + 1) * PATCHES] = parts[order[k]].astype(f32)[:PATCHES]


def feed_columns(layer):
    size = QUARTER if layer == 1 else CHUNK
    return [(2 * at, slice(at, at + size), size) for at in range(0, HALF_FF, size)]


def attn_columns():
    return [[FEED + (4 * k + c) * PAIR for c in range(4)] for k in range(STEPS)]


def shards_kernel(core, qkv, out, up, down, mine_out, sent_out):
    def fill(layer, half, target):
        for to, units, size in feed_columns(layer):
            units = slice(units.start + half * HALF_FF, units.stop + half * HALF_FF)
            target[:, to : to + size] = up[:, units].astype(low)
            target[:, to + size : to + 2 * size] = down[:, units].astype(low)
        for k, spots in enumerate(attn_columns()):
            at = slice(half * HALF + k * PAIR, half * HALF + (k + 1) * PAIR)
            for to, rows in zip(spots, (qkv[0, :, at], qkv[1, :, at], qkv[2, :, at], out[:, at])):
                target[:, to : to + PAIR] = rows.astype(low)

    for index in range(2):
        @pl.when(core[0] == index)
        def _():
            fill(index, index, mine_out)
            fill(index, 1 - index, sent_out)


def grads_kernel(
    core, first_half, second_half,
    qkv_out, out_out, up_out, down_out, qv_out, hidden_out, gains_out, biases_out, token_out, table_out,
):
    halves = first_half, second_half
    shared = first_half[:, LAYER : LAYER + D].astype(f32)

    def fill(layer, half, part):
        for at, units, size in feed_columns(layer):
            units = slice(units.start + half * HALF_FF, units.stop + half * HALF_FF)
            up_out[:, units] = part[:, at : at + size].astype(f32)
            down_out[:, units] = part[:, at + size : at + 2 * size].astype(f32)
        for k, spots in enumerate(attn_columns()):
            to = slice(half * HALF + k * PAIR, half * HALF + (k + 1) * PAIR)
            for c in range(3):
                qkv_out[c, :, to] = part[:, spots[c] : spots[c] + PAIR].astype(f32)
            out_out[:, to] = part[:, spots[3] : spots[3] + PAIR].astype(f32)

    for index in range(2):
        @pl.when(core[0] == index)
        def _():
            at = 9 * index
            gains_out[...] = shared[at : at + 2]
            biases_out[...] = shared[at + 2 : at + 6]
            token_out[...] = shared[18:19, index * HALF : (index + 1) * HALF]
            table_out[...] = shared[19 : 19 + GROUPS, index * HALF : (index + 1) * HALF]
            for h, half in enumerate(halves):
                fill(index, h, half)
                rows = half[:, LAYER : LAYER + D].astype(f32)
                for k in range(2):
                    qv_out[k : k + 1, h * HALF : (h + 1) * HALF] = rows[at + 6 : at + 7, k * HALF : (k + 1) * HALF]
                    hidden_out[:, h * HALF_FF + k * D : h * HALF_FF + (k + 1) * D] = rows[at + 7 + k : at + 8 + k]


def whole(array):
    return pl.BlockSpec(array.shape, lambda *_: (0,) * len(array.shape))


def shaped(shape, kind=f32):
    return jax.ShapeDtypeStruct(shape, kind)


def call(kernel, name, operands, outs, specs, micros, alias=None, scratch=(), limit=LIMIT):
    def spec(key, array):
        return specs.get(key) or whole(array)

    return pl.pallas_call(
        kernel,
        name=name,
        grid=(1,),
        in_specs=[spec(("in", k), a) for k, a in enumerate(operands)],
        out_specs=[spec(("out", k), a) for k, a in enumerate(outs)],
        out_shape=outs,
        scratch_shapes=scratch,
        input_output_aliases=alias or {},
        cost_estimate=pl.CostEstimate(flops=0, bytes_accessed=int(micros * 3.6e6), transcendentals=0),
        compiler_params=pltpu.CompilerParams(vmem_limit_bytes=limit),
    )(*operands)


SMALL = pl.BlockSpec(memory_space=pltpu.SMEM)
LEFT = pl.BlockSpec(memory_space=pl.ANY)


STREAM = shaped((ROWS, D))
STREAM_LOW = shaped((ROWS, D), low)


DMA = pltpu.SemaphoreType.DMA((STEPS,))
FEED_PARTS = pltpu.VMEM((STEPS, D, 2 * CHUNK), low)
ATTN_PARTS = pltpu.VMEM((STEPS, D, 4 * PAIR), low)
UPPER_PARTS = pltpu.VMEM((STEPS, ROWS, CHUNK), f32)
ATTN_KEPT = [STREAM_LOW, shaped((ROWS, 3 * HALF), low), shaped((STEPS, 8, ROWS)), shaped((ROWS, HALF), low), STREAM_LOW]
JOINED_GRADS = shaped((D, JOINED), low)


def attention_call(layer, entry, norms, offset, weights):
    second = layer == 1
    operands = (*entry, norms, offset, weights)
    return call(
        functools.partial(attention_kernel, second), f"attention_{layer}", operands, [STREAM, *ATTN_KEPT] if second else ATTN_KEPT,
        {("in", len(operands) - 1): LEFT}, 4, scratch=[ATTN_PARTS, DMA],
    )


def forward_call(stream, part, part_other, norms, bias_up, weights):
    return call(
        forward_kernel, "feed_0", (stream, part, part_other, norms, bias_up, weights),
        [STREAM, STREAM_LOW, shaped((ROWS, HALF_FF)), STREAM_LOW], {("in", 5): LEFT, ("out", 2): LEFT}, 4,
        scratch=[FEED_PARTS, UPPER_PARTS, DMA, DMA],
    )


def turn_call(slots, branch, stream, part, part_other, norms, bias_up, near, far):
    parts, sems = pltpu.VMEM((SIDE, D, 2 * QUARTER), low), pltpu.SemaphoreType.DMA((SIDE,))
    return call(
        turn_kernel, "feed_1", (slots, branch, stream, part, part_other, norms, bias_up, near, far),
        [JOINED_GRADS, STREAM, STREAM_LOW, STREAM_LOW, shaped((1, HALF_FF)), shaped((8, D))],
        {("in", 0): SMALL, ("in", 7): LEFT, ("in", 8): LEFT, ("out", 0): LEFT}, 9,
        scratch=[parts, parts, pltpu.VMEM((ROWS, D), low), *[pltpu.VMEM((ROWS, D), f32)] * 2, sems, sems],
    )


def backward_call(entry, normed, upper, weights, grads):
    return call(
        backward_kernel, "feed_back_0", (*entry, normed, upper, weights, grads),
        [JOINED_GRADS, STREAM_LOW, shaped((1, HALF_FF)), shaped((8, D)), STREAM_LOW],
        {("in", 6): LEFT, ("in", 7): LEFT, ("in", 8): LEFT, ("out", 0): LEFT}, 6, alias={8: 0},
        scratch=[FEED_PARTS, UPPER_PARTS, FEED_PARTS, DMA, DMA, DMA],
    )


def attention_back_call(layer, entry, branch, part, part_other, middle, norms, normed, packed, lse, context, weights, grads):
    second = layer == 1
    operands = (*entry, branch, part, part_other, middle, norms, normed, packed, lse, context, weights, *grads)
    outs = [JOINED_GRADS] if second else [shaped((2, 2, 2, SIDE, BLOCK, HALF), low)] * 2
    count, last = len(outs), len(operands) - 1
    specs = {("in", k): LEFT for k in ((last - 1, last) if second else (last,))}
    if not second:
        specs["in", 0] = SMALL
    specs.update({("out", k): LEFT for k in range(count)})
    made = call(
        functools.partial(attention_back_kernel, second), f"attention_back_{layer}", operands,
        [*outs, STREAM, STREAM_LOW, shaped((8, D)), shaped((1, 3 * HALF))], specs, 7, alias={last: 0} if second else None,
        scratch=[ATTN_PARTS, ATTN_PARTS, pltpu.VMEM((ROWS, 3 * PAIR), low), DMA, DMA],
    )
    return made[:count], made[count:]


def swap(value):
    return lax.ppermute(value, "section", SWAP)


def routes(axis, turn):
    pairs = []
    for place in range(2 * SIDE**3):
        spot = [place // SIDE**3, place // SIDE**2 % SIDE, place // SIDE % SIDE, place % SIDE]
        spot[axis + 1] ^= 1 if spot[0] == turn else 3
        pairs.append((place, ((spot[0] * SIDE + spot[1]) * SIDE + spot[2]) * SIDE + spot[3]))
    return pairs


def trade(value, axis, turn):
    return lax.ppermute(value, MESH, routes(axis, turn))


def add(*values):
    return functools.reduce(jnp.add, (v.astype(f32) for v in values)).astype(low)


def both_of(own, axis, turn):
    return jnp.stack([own, trade(own, axis, turn)])


def gather_first(own, axis):
    pair = both_of(own, axis, 0)
    return jnp.concatenate([pair, trade(pair, axis, 1)])


def gather_second(own, axis):
    pair = both_of(own, axis, 0)
    return pair, trade(pair, axis, 1)


def halves_of(kept, got):
    middle = kept.shape[0] // 2
    return add(kept[:middle], got[:middle]), add(kept[middle:], got[middle:])


tied = lax.optimization_barrier


def per_device(
    patches, mask_flags, image_tags, mask_token, group_table, qkv_weight, query_value_bias, out_weight,
    up_weight, hidden_bias, down_weight, norm_gains, norm_biases, cotangent,
):
    place = lax.axis_index("heads")
    core = lax.axis_index("section")
    first = core == 0

    x, y = lax.axis_index("dp") // SIDE, lax.axis_index("dp") % SIDE
    flips = jnp.where(first, jnp.array([0, 1, 3, 2], jnp.int32), jnp.array([0, 3, 1, 2], jnp.int32))
    slots = jnp.concatenate([x ^ flips, y ^ flips, place ^ flips])
    order = jnp.argmax((place ^ flips)[None, :] == jnp.arange(SIDE, dtype=jnp.int32)[:, None], axis=1).astype(jnp.int32)

    rows = qkv_weight.shape[1]
    mine, other = call(
        shards_kernel, "shards",
        (core.reshape(1), qkv_weight[0].transpose(1, 0, 2), out_weight[0].T, up_weight[0], down_weight[0].T),
        [shaped((rows, LAYER), low)] * 2, {("in", 0): SMALL}, 2, limit=ALL,
    )
    other = swap(other)
    zero, one = jnp.where(first, mine, other), jnp.where(first, other, mine)

    shard = jnp.concatenate([zero, one[:, FEED:]], axis=1)
    weights = lax.all_gather(shard, "dp", axis=0, tiled=True)
    quarter = lax.dynamic_slice_in_dim(one, place * 2 * QUARTER, 2 * QUARTER, 1)
    near = gather_first(quarter[:, :QUARTER], 0), gather_first(quarter[:, QUARTER:], 1)
    near = jnp.stack([*gather_second(near[0], 1), *gather_second(near[1], 0)])
    near = both_of(near, 2, 0)
    far = trade(near, 2, 1)
    later = (patches, mask_flags, image_tags, mask_token, group_table, cotangent, norm_gains, norm_biases, query_value_bias, hidden_bias)
    later, _ = tied((later, near))
    patches, mask_flags, image_tags, mask_token, group_table, cotangent, norm_gains, norm_biases, query_value_bias, hidden_bias = later

    def half_of(vector):
        return jnp.where(first, vector[..., : vector.shape[-1] // 2], vector[..., vector.shape[-1] // 2 :])

    vectors = lax.all_gather(
        jnp.concatenate([norm_gains[0], norm_biases[0], query_value_bias[0], hidden_bias[0].reshape(4, D)]),
        "section", axis=0,
    )
    norms, offsets, bias_ups = [], [], []
    for layer in range(2):
        v = vectors[layer]
        norms.append(jnp.pad(v[:6], ((0, 2), (0, 0))))
        query, value = half_of(v[6:8]).reshape(2, STEPS, PAIR)
        offsets.append(jnp.stack([query, jnp.zeros_like(query), value], axis=1).reshape(1, 3 * HALF))
        bias_ups.append(half_of(v[8:12].reshape(1, FF)))

    def own(rows_of):
        return lax.dynamic_slice_in_dim(rows_of, place * PATCHES, PATCHES, 0)

    def padded(value):
        return jnp.pad(value, ((0, ROWS - PATCHES), (0, 0)))

    masked = lax.dynamic_slice_in_dim(mask_flags, place, 1, 0).reshape(PATCHES, 1).astype(f32)
    tag = lax.dynamic_slice_in_dim(image_tags, place, 1, 0)
    onehot = (tag[:, None] == jnp.arange(GROUPS, dtype=jnp.int32)[None, :]).astype(f32)
    image_row = jnp.sum(onehot.T * group_table, axis=0, keepdims=True)
    stream_zero = padded(jnp.where(masked > 0, mask_token[None, :], own(patches).astype(f32)) + image_row)
    seed, masked = padded(own(cotangent)), padded(masked)

    normed, packed, lse, context, part = attention_call(0, (stream_zero,), norms[0], offsets[0], weights)
    middle, normed_two, upper, mixed = forward_call(stream_zero, part, swap(part), norms[0], bias_ups[0], weights)
    kept = (middle, norms[0], normed, packed, lse, context)
    stream_one, normed, packed, lse, context, part = attention_call(
        1, (middle, mixed, swap(mixed), norms[0][5:6]), norms[1], offsets[1], weights
    )
    grads, middle, mixed, part, bias_one, turn_rows = turn_call(
        slots, seed, stream_one, part, swap(part), norms[1], bias_ups[1], near, far
    )
    (grads,), (grad_middle, part, rows_one, sums_one) = attention_back_call(
        1, (), seed, part, swap(part), middle, norms[1], normed, packed, lse, context, weights, [grads]
    )
    grads, part, bias_zero, back_rows, branch = backward_call(
        (grad_middle, part, swap(part), stream_one, norms[1]), normed_two, upper, weights, grads
    )
    joined = lax.psum_scatter(grads, "dp", scatter_dimension=0, tiled=True)
    (kept, sent), (grad_middle, part, rows_zero, sums_zero) = attention_back_call(
        0, (slots,), branch, part, swap(part), *kept, weights, []
    )
    rows_out, vectors, _ = call(
        last_kernel, "last",
        (
            core.reshape(1), grad_middle, part, swap(part), stream_zero, norms[0], masked, tag, middle, mixed, swap(mixed),
            norms[1][5:6], rows_one, sums_one, turn_rows, bias_one, rows_zero, sums_zero, back_rows, bias_zero,
        ),
        [STREAM_LOW, shaped((BLOCK, D), low), shaped((32, D))], {("in", 0): SMALL, ("in", 7): SMALL}, 3, limit=ALL,
    )

    def trade_with(sent, vectors, axis, turn):
        got = trade(jnp.concatenate([sent.reshape(-1, BLOCK, HALF), vectors]), axis, turn)
        return got[:-2].reshape(sent.shape), add(vectors, got[-2:])

    vectors = jnp.stack([vectors[:, :HALF], vectors[:, HALF:]])
    got, vectors = trade_with(sent, vectors, 2, 1)
    kept, sent = halves_of(kept, got)
    got, vectors = trade_with(sent, vectors, 2, 0)
    kept, sent = add(kept[0], got[0])
    sent, rows_out = tied((sent, rows_out))
    got, vectors = trade_with(sent, vectors, 0, 1)
    kept, sent = halves_of(kept, got)
    got, vectors = trade_with(sent, vectors, 0, 0)
    kept, sent = halves_of(kept[0], got[0])
    ends = both_of(rows_out, 2, 0)
    ends = jnp.concatenate([ends, trade(ends, 2, 1)])
    got, vectors = trade_with(sent, vectors, 1, 1)
    kept, sent = halves_of(kept, got)
    got, vectors = trade_with(sent, vectors, 1, 0)
    quarter = add(kept[0], got[0])
    (ends_here,) = call(
        ends_kernel, "ends", (order, ends), [shaped((SIDE * PATCHES, D))], {("in", 0): SMALL}, 2, limit=ALL
    )
    joined, quarter, vectors, ends_here = tied((joined, quarter, vectors, ends_here))

    value = joined
    for turn in range(2):
        got = trade(jnp.concatenate([value, quarter], axis=1), 2, turn)
        value, quarter = add(value, got[:, : value.shape[1]]), jnp.concatenate([quarter, got[:, value.shape[1] :]], axis=1)
    quarter = quarter.reshape(rows, SIDE, HALF)
    kinds = [lax.dynamic_index_in_dim(quarter, order[k], 1, keepdims=False) for k in range(SIDE)]
    attn_zero = [kind[:, k * PAIR : (k + 1) * PAIR] for k in range(STEPS) for kind in kinds]
    zero = jnp.concatenate([value[:, FEED : 2 * FEED], *attn_zero, vectors[0], vectors[1]], axis=1)
    one = jnp.concatenate([value[:, :FEED], value[:, 2 * FEED :], vectors[0], vectors[1]], axis=1)
    mine = jnp.where(first, zero, one)
    other = swap(jnp.where(first, one, zero))
    grad_qkv, grad_out, grad_up, grad_down, grad_qv, grad_hidden, grad_gains, grad_biases, grad_token, grad_table = call(
        grads_kernel, "grads", (core.reshape(1), jnp.where(first, mine, other), jnp.where(first, other, mine)),
        [
            shaped((3, rows, D)), shaped((rows, D)), shaped((rows, FF)), shaped((rows, FF)), shaped((2, D)), shaped((1, FF)),
            shaped((2, D)), shaped((4, D)), shaped((1, HALF)), shaped((GROUPS, HALF)),
        ],
        {("in", 0): SMALL}, 2,
    )
    return (
        ends_here[None], grad_qkv.transpose(1, 0, 2)[None], grad_qv[None], grad_out.T[None], grad_up[None], grad_hidden,
        grad_down.T[None], grad_gains[None], grad_biases[None], grad_token[0], grad_table,
    )


def solution(mesh):
    in_specs = (
        P("dp", None), P("dp", None), P("dp"), P(), P(),
        P("section", "dp", None, None), P("section", None, None), P("section", None, "dp"),
        P("section", "dp", None), P("section", None), P("section", None, "dp"),
        P("section", None, None), P("section", None, None), P("dp", None),
    )
    out_specs = (
        P("section", "dp", None), P("section", "dp", None, None), P("section", None, None),
        P("section", None, "dp"), P("section", "dp", None), P("section", None), P("section", None, "dp"),
        P("section", None, None), P("section", None, None), P("section"), P(None, "section"),
    )
    return jax.shard_map(per_device, mesh=mesh, in_specs=in_specs, out_specs=out_specs, check_vma=False)
```
